32 devices in a mesh: line: 16 (over z, y, core), centroid: 2 (over x).
Axes of the slice: x: 2, y: 2, z: 4, core: 2. Of those that a mesh axis runs over, the one named last changes fastest.
Arguments:
- line_blocks: bfloat16 [256, 128, 768], P('line', 'centroid'), may hold values from -6 to 6
- line_counts: int32 [16], P('line'), may hold values from 0 to 2048, as said below
- destinations: int32 [256], P('line'), may hold values from 0 to 127, as said below
- centroids: bfloat16 [2048, 768], P(('centroid', 'line')), may hold values from -6 to 6
Outputs:
- nearest: float32 [128, 128], P('line', 'centroid')
- runner_up: float32 [128, 128], P('line', 'centroid')
The draws below stay inside these ranges and needn't reach their ends.
Inputs may be any that keep to these rules, and one draw needn't show every extreme that they name: `line_counts`: each count is a multiple of 128; the counts add up to 16384. `destinations`: among usable slots each balanced position is named exactly once, and position p is named by a slot of host p // 8 or of the host before it (host 16 - 1 before host 0). At most 8 usable slots of one host name positions of one host. Slots that are not usable hold arbitrary positions.
All inputs are finite; a program needn't handle non-finite values.
Results may differ from the reference program's by a relative error of at most 0.0003.
Values may be sent and summed in bfloat16 or wider, within the bound.
No kernel may reach another device: no remote copies, remote signals or barrier semaphores. Data moves between devices by JAX's collectives and lax.ppermute only.
A program may use at most 64 MiB of HBM per device.

```python
import jax
import jax.numpy as jnp
from jax import lax

D = 768
CENT_DEV = 64
BLK = 128
BAL = 8
K = 2048
N_LINE = 16
N_CENTROID = 2


def rebalance_plan(key):
    base_key = jax.random.fold_in(key, 31)
    key_offset, key_host, key_order, key_filler = jax.random.split(base_key, 4)
    slot_total = 2 * BAL
    host_ids = jnp.arange(N_LINE, dtype=jnp.int32)
    offsets = jax.random.randint(key_offset, (N_LINE, BAL), 0, 2)
    chosen_host = jax.random.randint(key_host, (), 0, N_LINE)
    relative = (host_ids - chosen_host) % N_LINE
    offsets = jnp.where(relative[:, None] == 0, 0, offsets)
    offsets = jnp.where(relative[:, None] == 1, 1, offsets)
    offsets = jnp.where(relative[:, None] == 2, 0, offsets)
    next_host = (host_ids + 1) % N_LINE
    place_ids = jnp.arange(BAL, dtype=jnp.int32)
    here_positions = host_ids[:, None] * BAL + place_ids[None, :]
    next_positions = next_host[:, None] * BAL + place_ids[None, :]
    candidates = jnp.concatenate([here_positions, next_positions], axis=1)
    eligible = jnp.concatenate([offsets == 0, offsets[next_host] == 1], axis=1).astype(jnp.int32)
    jitter = jax.random.randint(key_order, (N_LINE, slot_total), 0, 2 ** 20)
    ranking = (1 - eligible) * 2 ** 26 + jitter * slot_total + jnp.arange(slot_total, dtype=jnp.int32)[None, :]
    ordering = jnp.argsort(ranking, axis=1)
    block_count = jnp.sum(eligible, axis=1)
    picked = jnp.take_along_axis(candidates, ordering, axis=1)
    filler = jax.random.randint(key_filler, (N_LINE, slot_total), 0, N_LINE * BAL)
    slot_ids = jnp.arange(slot_total, dtype=jnp.int32)
    assigned = jnp.where(slot_ids[None, :] < block_count[:, None], picked, filler)
    return ((block_count * BLK).astype(jnp.int32), assigned.reshape(-1).astype(jnp.int32))


def lines_and_bank(key):
    counts, assigned = rebalance_plan(key)
    float_key = jax.random.fold_in(key, 57)
    key_lines, key_bank, key_place, key_row, key_noise, key_inner = jax.random.split(float_key, 6)
    slot_total = 2 * BAL
    all_slots = N_LINE * slot_total
    shard_count = N_LINE * N_CENTROID
    bank_total = CENT_DEV * shard_count
    lines = jnp.clip(jax.random.normal(key_lines, (all_slots, BLK, D), jnp.float32), -3.75, 3.75)
    bank = jnp.clip(jax.random.normal(key_bank, (bank_total, D), jnp.float32), -3.75, 3.75)
    flat_ids = jnp.arange(all_slots, dtype=jnp.int32)
    usable = flat_ids % slot_total * BLK < counts[flat_ids // slot_total]
    positions = jnp.arange(N_LINE * BAL, dtype=jnp.int32)
    matching = (usable[None, :] & (assigned[None, :] == positions[:, None])).astype(jnp.int32)
    slot_of_position = jnp.sum(matching * flat_ids[None, :], axis=1)
    planted_position = jax.random.randint(key_place, (shard_count,), 0, N_LINE * BAL)
    planted_row = jax.random.randint(key_row, (shard_count,), 0, BLK)
    source_slot = slot_of_position[planted_position]
    loud_mask = jnp.zeros((all_slots, BLK), jnp.float32).at[source_slot, planted_row].max(1.0)
    lines = jnp.clip(lines * (1.0 + 0.6 * loud_mask[:, :, None]), -6.0, 6.0)
    copies = lines[source_slot, planted_row] + 0.05 * jax.random.normal(key_noise, (shard_count, D), jnp.float32)
    inner_row = jax.random.randint(key_inner, (shard_count,), 0, CENT_DEV)
    chosen = jnp.arange(CENT_DEV, dtype=jnp.int32)[None, :] == inner_row[:, None]
    shards = bank.reshape(shard_count, CENT_DEV, D)
    shards = jnp.where(chosen[:, :, None], copies[:, None, :], shards)
    bank = jnp.clip(shards.reshape(bank_total, D), -6.0, 6.0)
    return (lines, bank)


def draw_line_blocks(key, part):
    return lines_and_bank(key)[0].astype(jnp.bfloat16)


def draw_centroids(key, part):
    return lines_and_bank(key)[1].astype(jnp.bfloat16)


def draw_line_counts(key, part):
    return rebalance_plan(key)[0]


def draw_destinations(key, part):
    return rebalance_plan(key)[1]


def setup_inputs(seed: int = 0) -> dict:
    streams_of = jax.random.split(jax.random.key(seed), 5)
    return {
        "line_blocks": draw_line_blocks(jax.random.fold_in(streams_of[4], 71), 0),
        "line_counts": draw_line_counts(jax.random.fold_in(streams_of[4], 71), 0),
        "destinations": draw_destinations(jax.random.fold_in(streams_of[4], 71), 0),
        "centroids": draw_centroids(jax.random.fold_in(streams_of[4], 71), 0),
    }


HUGE_DISTANCE = 3.0e38


def second_smallest(values, along):
    lowest = jnp.min(values, axis=along, keepdims=True)
    tie_count = jnp.sum((values == lowest).astype(jnp.int32), axis=along)
    others = jnp.min(jnp.where(values > lowest, values, HUGE_DISTANCE), axis=along)
    return jnp.where(tie_count >= 2, jnp.squeeze(lowest, along), others)


def combine(earlier, later):
    lowest = jnp.minimum(earlier[0], later[0])
    runner = jnp.minimum(jnp.minimum(jnp.maximum(earlier[0], later[0]), earlier[1]), later[1])
    return (lowest, runner)


def reference(line_blocks, line_counts, destinations, centroids):
    slot_total = 2 * BAL
    flat_ids = jnp.arange(N_LINE * slot_total, dtype=jnp.int32)
    slot_ids = flat_ids % slot_total
    host_ids = flat_ids // slot_total
    usable = slot_ids * BLK < line_counts[host_ids]
    targets = jnp.where(usable, destinations, N_LINE * BAL).astype(jnp.int32)
    placed = jax.ops.segment_sum(line_blocks.astype(jnp.float32), targets, num_segments=N_LINE * BAL + 1)[:-1]
    balanced_rows = placed.reshape(-1, D)
    line_norms = jnp.sum(balanced_rows * balanced_rows, axis=1)
    group_size = CENT_DEV * N_CENTROID
    bank_groups = centroids.astype(jnp.float32).reshape(K // group_size, group_size, D)

    def absorb_group(running, group):
        products = jnp.dot(balanced_rows, group.T, precision=lax.Precision.HIGHEST)
        bank_norms = jnp.sum(group * group, axis=1)
        distance = (line_norms[:, None] + bank_norms[None, :] - 2.0 * products) / D
        return combine(running, (jnp.min(distance, axis=1), second_smallest(distance, 1))), None

    line_total = balanced_rows.shape[0]
    starting = (jnp.full((line_total,), HUGE_DISTANCE, jnp.float32), jnp.full((line_total,), HUGE_DISTANCE, jnp.float32))
    final, unused = lax.scan(absorb_group, starting, bank_groups)
    return final[0].reshape(N_LINE * BAL, BLK), final[1].reshape(N_LINE * BAL, BLK)
```

```python
import functools

import jax
import jax.numpy as jnp
from jax import lax
from jax.experimental import pallas as pl
from jax.experimental.pallas import tpu as pltpu
from jax.sharding import PartitionSpec as P

HUGE_DISTANCE = 3e38
AXES = ("line", "centroid")
GROUP_LINES = 256
BANK_TILE = 512
SUBLANES = 8
VMEM_LIMIT = 24 * 2**20


def moved(value, target):
    hosts, columns = (lax.axis_size(axis) for axis in AXES)
    route = []
    for host in range(hosts):
        for column in range(columns):
            to = target(host, column)
            if to is not None:
                route.append((host * columns + column, to[0] % hosts * columns + to[1]))
    return lax.ppermute(value, AXES, route)


def across(axis, bit):
    if axis == "line":
        return lambda host, column: (host ^ 1 << bit, column)
    return lambda host, column: (host, column ^ 1 << bit)


def by_parity(even, odd):
    return lambda host, column: (odd if host & 1 else even)(host, column)


def fold(first, second, value):
    second = jnp.minimum(second, jnp.maximum(first, value))
    return jnp.minimum(first, value), second


def line_groups(lines, slots):
    per_slot = lines // slots
    return max(1, min(slots, GROUP_LINES // per_slot))


def norm_kernel(own_ref, partner_ref, norms_ref):
    lines, features = own_ref.shape
    ones = jnp.ones((SUBLANES, features), jnp.bfloat16)
    step = min(lines, GROUP_LINES)
    for part, ref in enumerate((own_ref, partner_ref)):
        for at in range(0, lines, step):
            wide = ref[at : at + step, :].astype(jnp.float32)
            square = wide * wide
            high = square.astype(jnp.bfloat16)
            low = (square - high.astype(jnp.float32)).astype(jnp.bfloat16)
            total = sum(
                lax.dot_general(
                    ones, half, (((1,), (1,)), ((), ())), preferred_element_type=jnp.float32
                )
                for half in (high, low)
            )
            norms_ref[:, part * lines + at : part * lines + at + step] = total


def line_norms(own, partner):
    lines, features = own.shape
    return pl.pallas_call(
        norm_kernel,
        out_shape=jax.ShapeDtypeStruct((SUBLANES, 2 * lines), jnp.float32),
        compiler_params=pltpu.CompilerParams(vmem_limit_bytes=VMEM_LIMIT),
        cost_estimate=pl.CostEstimate(
            flops=4 * SUBLANES * lines * features,
            bytes_accessed=4 * lines * features,
            transcendentals=0,
        ),
        name="line_norms",
    )(own, partner)


def absorb_kernel(slots, block_rows, counts_ref, bank_ref, own_ref, partner_ref, *rest):
    first_in, second_in, first_ref, second_ref = rest
    lines = own_ref.shape[0]
    per_slot = lines // slots
    group = line_groups(lines, slots)
    step = group * per_slot

    @pl.when(pl.program_id(0) == 0)
    def start():
        first_ref[...] = first_in[...]
        second_ref[...] = second_in[...]

    wide = bank_ref[...].astype(jnp.float32)
    bank_norms = jnp.sum(wide * wide, axis=1, keepdims=True)
    scaled = bank_ref[...] * jnp.array(-2, jnp.bfloat16)
    for part, ref in enumerate((own_ref, partner_ref)):
        for index in range(slots // group):

            @pl.when(index * group * block_rows < counts_ref[part])
            def work(part=part, ref=ref, index=index):
                products = lax.dot_general(
                    scaled,
                    ref[index * step : (index + 1) * step, :],
                    (((1,), (1,)), ((), ())),
                    preferred_element_type=jnp.float32,
                )
                distance = products + bank_norms
                at = slice(part * lines + index * step, part * lines + (index + 1) * step)
                first, second = first_ref[:, at], second_ref[:, at]
                for row in range(0, distance.shape[0], SUBLANES):
                    first, second = fold(first, second, distance[row : row + SUBLANES])
                first_ref[:, at] = first
                second_ref[:, at] = second


def absorb(running, bank, counts, own, partner, slots, block_rows):
    lines, features = own.shape
    centroids = bank.shape[0]
    tile = min(centroids, BANK_TILE)
    whole = lambda index: (0, 0)
    lines_spec = pl.BlockSpec((lines, features), whole)
    state_spec = pl.BlockSpec((SUBLANES, 2 * lines), whole)
    state = jax.ShapeDtypeStruct((SUBLANES, 2 * lines), jnp.float32)
    return pl.pallas_call(
        functools.partial(absorb_kernel, slots, block_rows),
        grid=(centroids // tile,),
        in_specs=[
            pl.BlockSpec(memory_space=pltpu.SMEM),
            pl.BlockSpec((tile, features), lambda index: (index, 0)),
            lines_spec,
            lines_spec,
            state_spec,
            state_spec,
        ],
        out_specs=(state_spec, state_spec),
        out_shape=(state, state),
        input_output_aliases={4: 0, 5: 1},
        compiler_params=pltpu.CompilerParams(vmem_limit_bytes=VMEM_LIMIT),
        cost_estimate=pl.CostEstimate(
            flops=4 * lines * centroids * features,
            bytes_accessed=4 * lines * features + 2 * centroids * features,
            transcendentals=0,
        ),
        name="absorb",
    )(counts, bank, own, partner, *running)


def reduce_kernel(features, first_in, second_in, norms_ref, own_ref, partner_ref):
    first, second = first_in[...], second_in[...]
    lowest, runner = first[:1], second[:1]
    for row in range(1, SUBLANES):
        low, high = first[row : row + 1], second[row : row + 1]
        runner = jnp.minimum(jnp.minimum(runner, high), jnp.maximum(lowest, low))
        lowest = jnp.minimum(lowest, low)
    norms = norms_ref[:1]
    lines = norms.shape[1] // 2
    both = [(value + norms) / features for value in (lowest, runner)]
    for row, value in enumerate(both):
        own_ref[row : row + 1, :] = value[:, :lines]
        partner_ref[row : row + 1, :] = value[:, lines:]


def reduced(running, norms, features):
    lines = norms.shape[1] // 2
    part = jax.ShapeDtypeStruct((2, lines), jnp.float32)
    return pl.pallas_call(
        functools.partial(reduce_kernel, features),
        out_shape=(part, part),
        name="reduced",
    )(*running, norms)


def scatter_kernel(block_rows, base_ref, count_ref, to_ref, mine_ref, returned_ref, keep_ref, send_ref):
    slots = to_ref.shape[0]
    places, per_slot = keep_ref.shape[1:]
    mine, returned = mine_ref[...], returned_ref[...]
    lowest = jnp.minimum(mine[:1], returned[:1])
    runner = jnp.minimum(
        jnp.minimum(mine[1:], returned[1:]), jnp.maximum(mine[:1], returned[:1])
    )
    keep_ref[...] = jnp.full(keep_ref.shape, HUGE_DISTANCE, jnp.float32)
    send_ref[...] = jnp.full(send_ref.shape, HUGE_DISTANCE, jnp.float32)
    for slot in range(slots):
        usable = slot * block_rows < count_ref[0]
        for ref, base in ((keep_ref, base_ref[0]), (send_ref, base_ref[1])):
            place = to_ref[slot] - base
            inside = jnp.logical_and(place >= 0, place < places)

            @pl.when(jnp.logical_and(usable, inside))
            def put(ref=ref, place=place, slot=slot):
                for row, value in enumerate((lowest, runner)):
                    ref[row, pl.ds(place, 1), :] = value[
                        :, slot * per_slot : (slot + 1) * per_slot
                    ]


def scattered(mine, returned, bases, line_counts, destinations, places, block_rows):
    slots = destinations.shape[0]
    per_slot = mine.shape[1] // slots
    placed = jax.ShapeDtypeStruct((2, places, per_slot), jnp.float32)
    smem = pl.BlockSpec(memory_space=pltpu.SMEM)
    vmem = pl.BlockSpec(memory_space=pltpu.VMEM)
    return pl.pallas_call(
        functools.partial(scatter_kernel, block_rows),
        in_specs=[smem, smem, smem, vmem, vmem],
        out_shape=(placed, placed),
        name="scattered",
    )(bases, line_counts, destinations, mine, returned)


def doubled(piece, bits):
    for axis, bit in bits:
        piece = jnp.concatenate([piece, moved(piece, across(axis, bit))], axis=0)
    return piece


def shards(line_blocks, line_counts, destinations, centroids):
    hosts, columns = (lax.axis_size(axis) for axis in AXES)
    host = lax.axis_index("line")
    slots, sub_rows, features = line_blocks.shape
    block_rows = sub_rows * columns
    places = slots // 2
    own = line_blocks.reshape(slots * sub_rows, features)
    partner_of = across("line", 0)
    partner = moved(own, partner_of)
    counts = jnp.concatenate([line_counts, moved(line_counts, partner_of)])

    far = [("line", bit) for bit in range(2, hosts.bit_length() - 1)]
    far += [("centroid", bit) for bit in range(1, columns.bit_length() - 1)]
    sets = [
        doubled(centroids, far[:-1]),
        doubled(moved(centroids, across(*far[-1])), far[:-1]),
    ]
    by_line, by_column = across("line", 1), across("centroid", 0)
    norms = line_norms(own, partner)
    running = (jnp.full((SUBLANES, norms.shape[1]), HUGE_DISTANCE, jnp.float32),) * 2
    for held in sets:
        near = moved(held, by_parity(by_column, by_line))
        side = moved(held, by_parity(by_line, by_column))
        corner = moved(near, by_parity(by_line, by_column))
        for bank in (held, near, side, corner):
            running = absorb(running, bank, counts, own, partner, slots, block_rows)

    mine, theirs = reduced(running, norms, features)
    returned = moved(theirs, partner_of)
    bases = jnp.stack([host, (host + 1) % hosts]).astype(jnp.int32) * places
    keep, send = scattered(
        mine, returned, bases, line_counts, destinations, places, block_rows
    )
    arrived = moved(send, lambda at, column: (at + 1, column))
    final = jnp.minimum(keep, arrived)
    return (final[0], final[1])


def solution(mesh):
    in_specs = (P("line", "centroid", None), P("line"), P("line"), P(("centroid", "line"), None))
    out_specs = (P("line", "centroid"), P("line", "centroid"))
    return jax.shard_map(shards, mesh=mesh, in_specs=in_specs, out_specs=out_specs, check_vma=False)
```

```python
import functools

import jax
import jax.numpy as jnp
from jax import lax
from jax.experimental import pallas as pl
from jax.experimental.pallas import tpu as pltpu
from jax.sharding import PartitionSpec as P

HUGE_DISTANCE = 3e38
AXES = ("line", "centroid")
BANK_TILE = 512
LINE_STEP = 1024
SUBLANES = 8
VMEM_LIMIT = 16 * 2**20
VMEM = pl.BlockSpec(memory_space=pltpu.VMEM)
SMEM = pl.BlockSpec(memory_space=pltpu.SMEM)


def moved(value, target):
    hosts, columns = (lax.axis_size(axis) for axis in AXES)
    route = []
    for host in range(hosts):
        for column in range(columns):
            to = target(host, column)
            route.append((host * columns + column, to[0] % hosts * columns + to[1]))
    return lax.ppermute(value, AXES, route)


def across(axis, bit):
    if axis == "line":
        return lambda host, column: (host ^ 1 << bit, column)
    return lambda host, column: (host, column ^ 1 << bit)


def by_parity(even, odd):
    return lambda host, column: (odd if host & 1 else even)(host, column)


def call(body, outs, operands, spaces, flops=0, scratch=(), aliases={}, name=None):
    traffic = sum(value.size * value.dtype.itemsize for value in operands)
    return pl.pallas_call(
        body,
        in_specs=list(spaces),
        out_specs=(VMEM,) * len(outs),
        out_shape=outs,
        scratch_shapes=list(scratch),
        input_output_aliases=aliases,
        compiler_params=pltpu.CompilerParams(vmem_limit_bytes=VMEM_LIMIT),
        cost_estimate=pl.CostEstimate(flops=flops, bytes_accessed=traffic, transcendentals=0),
        name=name,
    )(*operands)


def contract(left, right):
    return lax.dot_general(
        left, right, (((1,), (1,)), ((), ())), preferred_element_type=jnp.float32
    )


def fold(first, second, value):
    second = jnp.minimum(second, jnp.maximum(first, value))
    return jnp.minimum(first, value), second


def join(first, second, other_first, other_second):
    runner = jnp.minimum(jnp.minimum(second, other_second), jnp.maximum(first, other_first))
    return jnp.minimum(first, other_first), runner


def norm_kernel(own_ref, norms_ref):
    lines, features = own_ref.shape
    ones = jnp.ones((SUBLANES, features), jnp.bfloat16)
    step = min(lines, LINE_STEP)
    for at in range(0, lines, step):
        wide = own_ref[at : at + step, :].astype(jnp.float32)
        square = wide * wide
        high = square.astype(jnp.bfloat16)
        low = (square - high.astype(jnp.float32)).astype(jnp.bfloat16)
        norms_ref[:, at : at + step] = contract(ones, high) + contract(ones, low)


def line_norms(own):
    lines, features = own.shape
    out = jax.ShapeDtypeStruct((SUBLANES, lines), jnp.float32)
    return call(
        norm_kernel, (out,), (own,), (VMEM,), 32 * SUBLANES * lines * features, name="line_norms"
    )[0]


def prepared(banks):
    scaled = jnp.concatenate([bank * jnp.array(-2, jnp.bfloat16) for bank in banks], axis=0)
    wide = [bank.astype(jnp.float32) for bank in banks]
    norms = [jnp.sum(rows * rows, axis=1, keepdims=True) for rows in wide]
    return scaled, jnp.concatenate(norms, axis=0)


def absorbed(banks, lines, first, second):
    scaled, norms = prepared(banks)
    distance = contract(scaled, lines) + norms
    for row in range(0, distance.shape[0], SUBLANES):
        first, second = fold(first, second, distance[row : row + SUBLANES])
    return first, second


def tiles(bank_refs):
    plan, held, rows = [], [], 0
    for ref in bank_refs:
        tile = min(ref.shape[0], BANK_TILE)
        for at in range(0, ref.shape[0], tile):
            if rows + tile > BANK_TILE:
                plan.append(held)
                held, rows = [], 0
            held.append((ref, at, tile))
            rows += tile
    return plan + [held]


def absorb_kernel(line_count, bank_count, *refs):
    line_refs, refs = refs[:line_count], refs[line_count:]
    bank_refs, refs = refs[:bank_count], refs[bank_count:]
    for lines_ref, in_ref, out_ref in zip(line_refs, refs[:line_count], refs[line_count:]):
        lines = lines_ref.shape[0]
        step = min(lines, LINE_STEP)
        for at in range(0, lines, step):
            first, second = in_ref[:SUBLANES, at : at + step], in_ref[SUBLANES:, at : at + step]
            for group in tiles(bank_refs):
                banks = [ref[row : row + tile, :] for ref, row, tile in group]
                first, second = absorbed(banks, lines_ref[at : at + step, :], first, second)
            out_ref[:SUBLANES, at : at + step] = first
            out_ref[SUBLANES:, at : at + step] = second


def absorb(states, banks, line_sets):
    features = banks[0].shape[1]
    rows = sum(bank.shape[0] for bank in banks)
    total = sum(lines.shape[0] for lines in line_sets)
    count = len(line_sets)
    operands = (*line_sets, *banks, *states)
    return call(
        functools.partial(absorb_kernel, count, len(banks)),
        tuple(jax.ShapeDtypeStruct(state.shape, state.dtype) for state in states),
        operands,
        (VMEM,) * len(operands),
        2 * rows * total * features,
        aliases={count + len(banks) + i: i for i in range(count)},
        name="absorb",
    )


def last_kernel(slots, places, block_rows, bank_count, count_ref, to_ref, lines_ref, *refs):
    bank_refs, refs = refs[:bank_count], refs[bank_count:]
    mine_ref, returned_ref, norms_ref, keep_ref, send_ref, placed_ref = refs
    lines, features = lines_ref.shape
    per_slot = lines // slots
    hosts = lax.axis_size("line")
    host = lax.axis_index("line")
    following = lax.rem(host + 1, hosts)
    first, second = join(
        mine_ref[:SUBLANES], mine_ref[SUBLANES:], returned_ref[:SUBLANES], returned_ref[SUBLANES:]
    )
    for group in tiles(bank_refs):
        banks = [ref[row : row + tile, :] for ref, row, tile in group]
        first, second = absorbed(banks, lines_ref[...], first, second)
    lowest, runner = first[:1], second[:1]
    for row in range(1, SUBLANES):
        lowest, runner = join(lowest, runner, first[row : row + 1], second[row : row + 1])
    both = [(value + norms_ref[:1]) / features for value in (lowest, runner)]
    placed_ref[...] = jnp.full(placed_ref.shape, HUGE_DISTANCE, jnp.float32)
    for slot in range(slots):
        usable = slot * block_rows < count_ref[0]
        here = to_ref[slot] - host * places
        there = to_ref[slot] - following * places
        row = jnp.where(jnp.logical_and(there >= 0, there < places), places + there, 2 * places)
        row = jnp.where(jnp.logical_and(here >= 0, here < places), here, row)
        row = jnp.where(usable, row, 2 * places)
        for index, value in enumerate(both):
            placed_ref[index, pl.ds(row, 1), :] = value[:, slot * per_slot : (slot + 1) * per_slot]
    keep_ref[...] = placed_ref[:, :places]
    send_ref[...] = placed_ref[:, places : 2 * places]


def last(line_counts, destinations, own, banks, mine, returned, norms, places, block_rows):
    slots = destinations.shape[0]
    lines, features = own.shape
    per_slot = lines // slots
    operands = (line_counts, destinations, own, *banks, mine, returned, norms)
    placed = jax.ShapeDtypeStruct((2, places, per_slot), jnp.float32)
    return call(
        functools.partial(last_kernel, slots, places, block_rows, len(banks)),
        (placed, placed),
        operands,
        (SMEM, SMEM) + (VMEM,) * (len(operands) - 2),
        2 * lines * features * sum(bank.shape[0] for bank in banks),
        scratch=(pltpu.VMEM((2, 2 * places + SUBLANES, per_slot), jnp.float32),),
        name="last",
    )


def final_kernel(keep_ref, arrived_ref, nearest_ref, runner_ref):
    for index, ref in enumerate((nearest_ref, runner_ref)):
        ref[...] = jnp.minimum(keep_ref[index], arrived_ref[index])


def final(keep, arrived):
    out = jax.ShapeDtypeStruct(keep.shape[1:], keep.dtype)
    return call(final_kernel, (out, out), (keep, arrived), (VMEM, VMEM), name="final")


def doubled(piece, bits):
    for axis, bit in bits:
        piece = jnp.concatenate([piece, moved(piece, across(axis, bit))], axis=0)
    return piece


def shards(line_blocks, line_counts, destinations, centroids):
    hosts, columns = (lax.axis_size(axis) for axis in AXES)
    slots, sub_rows, features = line_blocks.shape
    block_rows = sub_rows * columns
    places = slots // 2
    own = line_blocks.reshape(slots * sub_rows, features)
    partner_of = across("line", 0)
    partner = moved(own, partner_of)

    far = [("line", bit) for bit in range(2, hosts.bit_length() - 1)]
    far += [("centroid", bit) for bit in range(1, columns.bit_length() - 1)]
    distant = moved(centroids, across(*far[-1]))
    norms = line_norms(own)
    by_line, by_column = across("line", 1), across("centroid", 0)
    turned, straight = by_parity(by_line, by_column), by_parity(by_column, by_line)

    held_a = doubled(centroids, far[:-1])
    held_a, norms = lax.optimization_barrier((held_a, norms))
    near_a = moved(held_a, straight)
    distant, held_late = lax.optimization_barrier((distant, held_a))
    held_b = doubled(distant, far[:-1])
    side_a = moved(held_late, turned)

    empty = jnp.full((2 * SUBLANES, own.shape[0]), HUGE_DISTANCE, jnp.float32)
    states = absorb((empty, empty), (held_late,), (own, partner))
    held_b, states = lax.optimization_barrier((held_b, states))
    corner_a = moved(near_a, turned)
    near_b = moved(held_b, straight)
    side_b = moved(held_b, turned)
    corner_b = moved(near_b, turned)
    states = absorb(states, (near_a, held_b), (own, partner))
    states = absorb(states, (side_a, corner_a), (own, partner))
    states = absorb(states, (near_b, side_b), (own, partner))
    corner_b, states = lax.optimization_barrier((corner_b, states))
    returned = moved(states[1], partner_of)
    shared = moved(corner_b, partner_of)
    keep, send = last(
        line_counts,
        destinations,
        own,
        (corner_b, shared),
        states[0],
        returned,
        norms,
        places,
        block_rows,
    )
    arrived = moved(send, lambda host, column: (host + 1, column))
    return tuple(final(keep, arrived))


def solution(mesh):
    in_specs = (P("line", "centroid", None), P("line"), P("line"), P(("centroid", "line"), None))
    out_specs = (P("line", "centroid"), P("line", "centroid"))
    return jax.shard_map(shards, mesh=mesh, in_specs=in_specs, out_specs=out_specs, check_vma=False)
```

```python
import functools

import jax
import jax.numpy as jnp
from jax import lax
from jax.experimental import pallas as pl
from jax.experimental.pallas import tpu as pltpu
from jax.sharding import PartitionSpec as P

HUGE_DISTANCE = 3e38
AXES = ("line", "centroid")
BANK_TILE = 512
LINE_STEP = 1024
SUBLANES = 8
VMEM_LIMIT = 16 * 2**20
VMEM = pl.BlockSpec(memory_space=pltpu.VMEM)
SMEM = pl.BlockSpec(memory_space=pltpu.SMEM)


def moved(value, target):
    hosts, columns = (lax.axis_size(axis) for axis in AXES)
    route = []
    for host in range(hosts):
        for column in range(columns):
            to = target(host, column)
            if to is None:
                continue
            route.append((host * columns + column, to[0] % hosts * columns + to[1]))
    return lax.ppermute(value, AXES, route)


def across(axis, bit):
    if axis == "line":
        return lambda host, column: (host ^ 1 << bit, column)
    return lambda host, column: (host, column ^ 1 << bit)


def by_parity(even, odd):
    return lambda host, column: (odd if host & 1 else even)(host, column)


def call(body, outs, operands, spaces, flops=0, scratch=(), aliases={}, name=None):
    traffic = sum(value.size * value.dtype.itemsize for value in operands)
    return pl.pallas_call(
        body,
        in_specs=list(spaces),
        out_specs=(VMEM,) * len(outs),
        out_shape=outs,
        scratch_shapes=list(scratch),
        input_output_aliases=aliases,
        compiler_params=pltpu.CompilerParams(vmem_limit_bytes=VMEM_LIMIT),
        cost_estimate=pl.CostEstimate(flops=flops, bytes_accessed=traffic, transcendentals=0),
        name=name,
    )(*operands)


def contract(left, right):
    return lax.dot_general(
        left, right, (((1,), (1,)), ((), ())), preferred_element_type=jnp.float32
    )


def fold(first, second, value):
    second = jnp.minimum(second, jnp.maximum(first, value))
    return jnp.minimum(first, value), second


def join(first, second, other_first, other_second):
    runner = jnp.minimum(jnp.minimum(second, other_second), jnp.maximum(first, other_first))
    return jnp.minimum(first, other_first), runner


def norm_kernel(own_ref, norms_ref):
    lines, features = own_ref.shape
    ones = jnp.ones((SUBLANES, features), jnp.bfloat16)
    step = min(lines, LINE_STEP)
    for at in range(0, lines, step):
        wide = own_ref[at : at + step, :].astype(jnp.float32)
        square = wide * wide
        high = square.astype(jnp.bfloat16)
        low = (square - high.astype(jnp.float32)).astype(jnp.bfloat16)
        norms_ref[:, at : at + step] = contract(ones, high) + contract(ones, low)


def line_norms(own):
    lines, features = own.shape
    out = jax.ShapeDtypeStruct((SUBLANES, lines), jnp.float32)
    return call(
        norm_kernel, (out,), (own,), (VMEM,), 32 * SUBLANES * lines * features, name="line_norms"
    )[0]


def prepared(banks):
    scaled = jnp.concatenate([bank * jnp.array(-2, jnp.bfloat16) for bank in banks], axis=0)
    wide = [bank.astype(jnp.float32) for bank in banks]
    norms = [jnp.sum(rows * rows, axis=1, keepdims=True) for rows in wide]
    return scaled, jnp.concatenate(norms, axis=0)


def absorbed(banks, lines, first, second):
    scaled, norms = prepared(banks)
    distance = contract(scaled, lines) + norms
    for row in range(0, distance.shape[0], SUBLANES):
        first, second = fold(first, second, distance[row : row + SUBLANES])
    return first, second


def tiles(bank_refs):
    plan, held, rows = [], [], 0
    for ref in bank_refs:
        tile = min(ref.shape[0], BANK_TILE)
        for at in range(0, ref.shape[0], tile):
            if rows + tile > BANK_TILE:
                plan.append(held)
                held, rows = [], 0
            held.append((ref, at, tile))
            rows += tile
    return plan + [held]


def absorb_kernel(line_count, bank_count, *refs):
    line_refs, refs = refs[:line_count], refs[line_count:]
    bank_refs, refs = refs[:bank_count], refs[bank_count:]
    for lines_ref, in_ref, out_ref in zip(line_refs, refs[:line_count], refs[line_count:]):
        lines = lines_ref.shape[0]
        step = min(lines, LINE_STEP)
        for at in range(0, lines, step):
            first, second = in_ref[:SUBLANES, at : at + step], in_ref[SUBLANES:, at : at + step]
            for group in tiles(bank_refs):
                banks = [ref[row : row + tile, :] for ref, row, tile in group]
                first, second = absorbed(banks, lines_ref[at : at + step, :], first, second)
            out_ref[:SUBLANES, at : at + step] = first
            out_ref[SUBLANES:, at : at + step] = second


def absorb(states, banks, line_sets):
    features = banks[0].shape[1]
    rows = sum(bank.shape[0] for bank in banks)
    total = sum(lines.shape[0] for lines in line_sets)
    count = len(line_sets)
    operands = (*line_sets, *banks, *states)
    return call(
        functools.partial(absorb_kernel, count, len(banks)),
        tuple(jax.ShapeDtypeStruct(state.shape, state.dtype) for state in states),
        operands,
        (VMEM,) * len(operands),
        2 * rows * total * features,
        aliases={count + len(banks) + i: i for i in range(count)},
        name="absorb",
    )


def last_kernel(parity, places, block_rows, count_ref, to_ref, lines_ref, *refs):
    bank_refs, refs = refs[:2], refs[2:]
    mine_ref, returned_ref, norms_ref, _, keep_ref, send_ref, placed_ref = refs
    lines, features = lines_ref.shape
    slots = to_ref.shape[0]
    per_slot = lines // slots
    host = lax.axis_index("line")

    @pl.when(lax.rem(host, 2) == parity)
    def work():
        following = lax.rem(host + 1, lax.axis_size("line"))
        first, second = join(
            mine_ref[:SUBLANES],
            mine_ref[SUBLANES:],
            returned_ref[:SUBLANES],
            returned_ref[SUBLANES:],
        )
        for group in tiles(bank_refs):
            banks = [ref[row : row + tile, :] for ref, row, tile in group]
            first, second = absorbed(banks, lines_ref[...], first, second)
        lowest, runner = first[:1], second[:1]
        for row in range(1, SUBLANES):
            lowest, runner = join(lowest, runner, first[row : row + 1], second[row : row + 1])
        both = [(value + norms_ref[:1]) / features for value in (lowest, runner)]
        placed_ref[...] = jnp.full(placed_ref.shape, HUGE_DISTANCE, jnp.float32)
        for slot in range(slots):
            usable = slot * block_rows < count_ref[0]
            here = to_ref[slot] - host * places
            there = to_ref[slot] - following * places
            row = jnp.where(jnp.logical_and(there >= 0, there < places), places + there, 2 * places)
            row = jnp.where(jnp.logical_and(here >= 0, here < places), here, row)
            row = jnp.where(usable, row, 2 * places)
            for index, value in enumerate(both):
                placed_ref[index, pl.ds(row, 1), :] = value[:, slot * per_slot : (slot + 1) * per_slot]
        keep_ref[...] = placed_ref[:, :places]
        send_ref[...] = placed_ref[:, places : 2 * places]


def last(parity, keep, line_counts, destinations, own, banks, mine, returned, norms, block_rows):
    lines, features = own.shape
    places, per_slot = keep.shape[1:]
    operands = (line_counts, destinations, own, *banks, mine, returned, norms, keep)
    placed = jax.ShapeDtypeStruct(keep.shape, keep.dtype)
    return call(
        functools.partial(last_kernel, parity, places, block_rows),
        (placed, placed),
        operands,
        (SMEM, SMEM) + (VMEM,) * (len(operands) - 2),
        2 * lines * features * sum(bank.shape[0] for bank in banks),
        scratch=(pltpu.VMEM((2, 2 * places + SUBLANES, per_slot), jnp.float32),),
        aliases={len(operands) - 1: 0},
        name="last",
    )


def merge_kernel(placed_ref, arrived_ref, out_ref):
    @pl.when(lax.rem(lax.axis_index("line"), 2) == 0)
    def merge():
        out_ref[...] = jnp.minimum(placed_ref[...], arrived_ref[...])


def merged(placed, arrived):
    out = jax.ShapeDtypeStruct(placed.shape, placed.dtype)
    return call(
        merge_kernel, (out,), (placed, arrived), (VMEM,) * 2, 10**9, aliases={0: 0}, name="merged"
    )[0]


def final_kernel(placed_ref, arrived_ref, nearest_ref, runner_ref):
    even = lax.rem(lax.axis_index("line"), 2) == 0
    for index, ref in enumerate((nearest_ref, runner_ref)):

        @pl.when(even)
        def ready(index=index, ref=ref):
            ref[...] = placed_ref[index]

        @pl.when(jnp.logical_not(even))
        def merge(index=index, ref=ref):
            ref[...] = jnp.minimum(placed_ref[index], arrived_ref[index])


def final(placed, arrived):
    out = jax.ShapeDtypeStruct(placed.shape[1:], placed.dtype)
    return call(final_kernel, (out, out), (placed, arrived), (VMEM,) * 2, name="final")


def stacked(pieces):
    return jnp.concatenate(pieces, axis=0) if len(pieces) > 1 else pieces[0]


def doubled(pieces, bits):
    for axis, bit in bits:
        pieces = [*pieces, moved(stacked(pieces), across(axis, bit))]
    return pieces


def shards(line_blocks, line_counts, destinations, centroids):
    hosts, columns = (lax.axis_size(axis) for axis in AXES)
    slots, sub_rows, features = line_blocks.shape
    block_rows = sub_rows * columns
    places = slots // 2
    own = line_blocks.reshape(slots * sub_rows, features)
    partner_of = across("line", 0)
    partner = moved(own, partner_of)

    far = [("line", bit) for bit in range(2, hosts.bit_length() - 1)]
    far += [("centroid", bit) for bit in range(1, columns.bit_length() - 1)]
    by_line, by_column = across("line", 1), across("centroid", 0)
    turned, straight = by_parity(by_line, by_column), by_parity(by_column, by_line)

    distant = moved(centroids, across(*far[-1]))
    level = doubled([centroids], far[:-1])[1:]
    near = moved(centroids, straight)
    side = moved(centroids, turned)
    distant, near, side = lax.optimization_barrier((distant, near, side))
    beyond = doubled([distant], far[:-1])[1:]
    norms = line_norms(own)
    beyond, norms = lax.optimization_barrier((beyond, norms))
    near_level = moved(stacked([*level, distant]), straight)
    near_beyond = moved(stacked(beyond), straight)
    crossed_level = moved(stacked([near, *level, distant, *beyond]), turned)
    crossed_beyond = moved(stacked([near_level, near_beyond]), turned)

    lines = (own, partner)
    empty = jnp.full((2 * SUBLANES, own.shape[0]), HUGE_DISTANCE, jnp.float32)
    states = absorb((empty, empty), (centroids, near, side, *level), lines)
    states = absorb(states, (distant, near_level, *beyond), lines)
    mine, theirs = absorb(states, (near_beyond, crossed_level), lines)
    returned = moved(theirs, partner_of)
    crossed_beyond, mine = lax.optimization_barrier((crossed_beyond, mine))
    banks = (crossed_beyond, moved(crossed_beyond, partner_of))

    placed = jnp.zeros((2, places, sub_rows), jnp.float32)
    sends = [None, None]
    for parity in (1, 0):
        placed, sends[parity] = last(
            parity,
            placed,
            line_counts,
            destinations,
            own,
            banks,
            mine,
            returned,
            norms,
            block_rows,
        )
    to_even = moved(sends[1], lambda host, column: (host + 1, column))
    to_odd = moved(sends[0], partner_of)
    return tuple(final(merged(placed, to_even), to_odd))


def solution(mesh):
    in_specs = (P("line", "centroid", None), P("line"), P("line"), P(("centroid", "line"), None))
    out_specs = (P("line", "centroid"), P("line", "centroid"))
    return jax.shard_map(shards, mesh=mesh, in_specs=in_specs, out_specs=out_specs, check_vma=False)
```

```python
import functools

import jax
import jax.numpy as jnp
from jax import lax
from jax.experimental import pallas as pl
from jax.experimental.pallas import tpu as pltpu
from jax.sharding import PartitionSpec as P

HUGE_DISTANCE = 3e38
AXES = ("line", "centroid")
BANK_TILE = 512
LINE_STEP = 1024
SUBLANES = 8
VMEM_LIMIT = 16 * 2**20
VMEM = pl.BlockSpec(memory_space=pltpu.VMEM)
SMEM = pl.BlockSpec(memory_space=pltpu.SMEM)


def moved(value, target):
    hosts, columns = (lax.axis_size(axis) for axis in AXES)
    route = []
    for host in range(hosts):
        for column in range(columns):
            to = target(host, column)
            if to is None:
                continue
            route.append((host * columns + column, to[0] % hosts * columns + to[1]))
    return lax.ppermute(value, AXES, route)


def across(axis, bit):
    if axis == "line":
        return lambda host, column: (host ^ 1 << bit, column)
    return lambda host, column: (host, column ^ 1 << bit)


def by_parity(even, odd):
    return lambda host, column: (odd if host & 1 else even)(host, column)


def call(body, outs, operands, spaces, flops=0, scratch=(), aliases={}, name=None):
    traffic = sum(value.size * value.dtype.itemsize for value in operands)
    return pl.pallas_call(
        body,
        in_specs=list(spaces),
        out_specs=(VMEM,) * len(outs),
        out_shape=outs,
        scratch_shapes=list(scratch),
        input_output_aliases=aliases,
        compiler_params=pltpu.CompilerParams(vmem_limit_bytes=VMEM_LIMIT),
        cost_estimate=pl.CostEstimate(flops=flops, bytes_accessed=traffic, transcendentals=0),
        name=name,
    )(*operands)


def contract(left, right):
    return lax.dot_general(
        left, right, (((1,), (1,)), ((), ())), preferred_element_type=jnp.float32
    )


def fold(first, second, value):
    second = jnp.minimum(second, jnp.maximum(first, value))
    return jnp.minimum(first, value), second


def join(first, second, other_first, other_second):
    runner = jnp.minimum(jnp.minimum(second, other_second), jnp.maximum(first, other_first))
    return jnp.minimum(first, other_first), runner


def pack_kernel(slots, block_rows, count_ref, own_ref, partner_ref, packed_ref):
    lines = own_ref.shape[0]
    per_slot = lines // slots
    half = lines // 2
    packed_ref[:half, :] = own_ref[:half, :]
    for slot in range(slots // 2, slots):
        here = slice(slot * per_slot, (slot + 1) * per_slot)
        other = 3 * slots // 2 - 1 - slot
        theirs = slice(other * per_slot, (other + 1) * per_slot)
        usable = slot * block_rows < count_ref[...]
        packed_ref[here, :] = jnp.where(usable, own_ref[here, :], partner_ref[theirs, :])


def pack(line_counts, own, partner, slots, block_rows):
    return call(
        functools.partial(pack_kernel, slots, block_rows),
        (jax.ShapeDtypeStruct(own.shape, own.dtype),),
        (line_counts.reshape(1, 1), own, partner),
        (VMEM, VMEM, VMEM),
        name="pack",
    )[0]


def spread(ref, row, order=None):
    slots, per_slot = ref.shape
    for place in range(slots):
        slot = place if order is None else order[place]
        ref[slot : slot + 1, :] = row[:, place * per_slot : (place + 1) * per_slot]


def norm_kernel(own_ref, norms_ref):
    slots, per_slot = norms_ref.shape
    lines, features = own_ref.shape
    ones = jnp.ones((SUBLANES, features), jnp.bfloat16)
    wide = own_ref[...].astype(jnp.float32)
    square = wide * wide
    high = square.astype(jnp.bfloat16)
    low = (square - high.astype(jnp.float32)).astype(jnp.bfloat16)
    spread(norms_ref, (contract(ones, high) + contract(ones, low))[:1])


def line_norms(own, slots):
    lines, features = own.shape
    out = jax.ShapeDtypeStruct((slots, lines // slots), jnp.float32)
    return call(
        norm_kernel, (out,), (own,), (VMEM,), 32 * SUBLANES * lines * features, name="line_norms"
    )[0]


def prepared(banks):
    scaled = jnp.concatenate([bank * jnp.array(-2, jnp.bfloat16) for bank in banks], axis=0)
    wide = [bank.astype(jnp.float32) for bank in banks]
    norms = [jnp.sum(rows * rows, axis=1, keepdims=True) for rows in wide]
    return scaled, jnp.concatenate(norms, axis=0)


def absorbed(banks, lines, first, second):
    scaled, norms = prepared(banks)
    distance = contract(scaled, lines) + norms
    for row in range(0, distance.shape[0], SUBLANES):
        first, second = fold(first, second, distance[row : row + SUBLANES])
    return first, second


def tiles(bank_refs):
    plan, held, rows = [], [], 0
    for ref in bank_refs:
        tile = min(ref.shape[0], BANK_TILE)
        for at in range(0, ref.shape[0], tile):
            if rows + tile > BANK_TILE:
                plan.append(held)
                held, rows = [], 0
            held.append((ref, at, tile))
            rows += tile
    return plan + [held]


def absorb_kernel(line_count, bank_count, give, *refs):
    line_refs, refs = refs[:line_count], refs[line_count:]
    bank_refs, refs = refs[:bank_count], refs[bank_count:]
    for lines_ref, in_ref, out_ref in zip(line_refs, refs[:line_count], refs[line_count:]):
        lines = lines_ref.shape[0]
        if in_ref is not refs[0]:
            lines //= 2
        step = min(lines, LINE_STEP)
        for at in range(0, lines, step):
            first, second = in_ref[:SUBLANES, at : at + step], in_ref[SUBLANES:, at : at + step]
            for group in tiles(bank_refs):
                banks = [ref[row : row + tile, :] for ref, row, tile in group]
                first, second = absorbed(banks, lines_ref[at : at + step, :], first, second)
            out_ref[:SUBLANES, at : at + step] = first
            out_ref[SUBLANES:, at : at + step] = second
    if give:
        mine_ref, theirs_ref = refs[line_count:]
        half = mine_ref.shape[1] // 2
        theirs_ref[:, half:] = mine_ref[:, half:]


def absorb(states, banks, line_sets, give=False):
    features = banks[0].shape[1]
    rows = sum(bank.shape[0] for bank in banks)
    total = sum(lines.shape[0] for lines in line_sets)
    count = len(line_sets)
    operands = (*line_sets, *banks, *states)
    return call(
        functools.partial(absorb_kernel, count, len(banks), give),
        tuple(jax.ShapeDtypeStruct(state.shape, state.dtype) for state in states),
        operands,
        (VMEM,) * len(operands),
        2 * rows * total * features,
        aliases={count + len(banks) + i: i for i in range(count)},
        name="absorb",
    )


def folded(first, second):
    rows = first.shape[0]
    while rows > 1:
        rows //= 2
        first, second = join(first[:rows], second[:rows], first[rows:], second[rows:])
    return first, second


def last_kernel(parity, block_rows, count_ref, to_ref, lines_ref, *refs):
    bank_refs, refs = refs[:2], refs[2:]
    mine_ref, returned_ref, norms_ref, _, keep_ref, send_ref, slot_ref = refs
    lines, features = lines_ref.shape
    slots, per_slot = norms_ref.shape
    places = keep_ref.shape[1]
    host = lax.axis_index("line")

    @pl.when(lax.rem(host, 2) == parity)
    def work():
        given = folded(returned_ref[:SUBLANES], returned_ref[SUBLANES:])
        order = [*range(slots // 2), *reversed(range(slots // 2, slots))]
        for index, value in enumerate(given):
            spread(slot_ref.at[2 + index], value, order)
        first, second = mine_ref[:SUBLANES], mine_ref[SUBLANES:]
        for group in tiles(bank_refs):
            banks = [ref[row : row + tile, :] for ref, row, tile in group]
            first, second = absorbed(banks, lines_ref[...], first, second)
        for index, value in enumerate(folded(first, second)):
            spread(slot_ref.at[index], value)
        both = join(slot_ref[0], slot_ref[1], slot_ref[2], slot_ref[3])
        both = [(value + norms_ref[...]) / features for value in both]

        following = lax.rem(host + 1, lax.axis_size("line"))
        slot = lax.broadcasted_iota(jnp.int32, (slots, slots), 0)
        across_slots = lax.broadcasted_iota(jnp.int32, (slots, slots), 1)
        to = jnp.where(slot == across_slots, to_ref[...], 0)
        to = jnp.sum(to, axis=1, keepdims=True)
        usable = slot[:, :1] * block_rows < count_ref[...]
        for ref, base in ((keep_ref, host * places), (send_ref, following * places)):
            place = jnp.where(usable, to - base, -1)
            for row in range(places):
                chosen = place == row
                for index, value in enumerate(both):
                    picked = jnp.where(chosen, value, HUGE_DISTANCE)
                    ref[index, row : row + 1, :] = jnp.min(picked, axis=0, keepdims=True)


def last(parity, keep, line_counts, destinations, own, banks, mine, returned, norms, block_rows):
    lines, features = own.shape
    counts, to = line_counts.reshape(1, 1), destinations.reshape(1, -1)
    operands = (counts, to, own, *banks, mine, returned, norms, keep)
    placed = jax.ShapeDtypeStruct(keep.shape, keep.dtype)
    return call(
        functools.partial(last_kernel, parity, block_rows),
        (placed, placed),
        operands,
        (VMEM,) * len(operands),
        2 * lines * features * sum(bank.shape[0] for bank in banks),
        scratch=(pltpu.VMEM((4, *norms.shape), jnp.float32),),
        aliases={len(operands) - 1: 0},
        name="last",
    )


def merge_kernel(placed_ref, arrived_ref, out_ref):
    @pl.when(lax.rem(lax.axis_index("line"), 2) == 0)
    def merge():
        out_ref[...] = jnp.minimum(placed_ref[...], arrived_ref[...])


def merged(placed, arrived):
    out = jax.ShapeDtypeStruct(placed.shape, placed.dtype)
    return call(
        merge_kernel, (out,), (placed, arrived), (VMEM,) * 2, 10**9, aliases={0: 0}, name="merged"
    )[0]


def final_kernel(placed_ref, arrived_ref, nearest_ref, runner_ref):
    even = lax.rem(lax.axis_index("line"), 2) == 0
    for index, ref in enumerate((nearest_ref, runner_ref)):

        @pl.when(even)
        def ready(index=index, ref=ref):
            ref[...] = placed_ref[index]

        @pl.when(jnp.logical_not(even))
        def merge(index=index, ref=ref):
            ref[...] = jnp.minimum(placed_ref[index], arrived_ref[index])


def final(placed, arrived):
    out = jax.ShapeDtypeStruct(placed.shape[1:], placed.dtype)
    return call(final_kernel, (out, out), (placed, arrived), (VMEM,) * 2, name="final")


def stacked(pieces):
    return jnp.concatenate(pieces, axis=0) if len(pieces) > 1 else pieces[0]


def doubled(pieces, bits):
    for axis, bit in bits:
        pieces = [*pieces, moved(stacked(pieces), across(axis, bit))]
    return pieces


def shards(line_blocks, line_counts, destinations, centroids):
    hosts, columns = (lax.axis_size(axis) for axis in AXES)
    slots, sub_rows, features = line_blocks.shape
    block_rows = sub_rows * columns
    places = slots // 2
    own = line_blocks.reshape(slots * sub_rows, features)
    partner_of = across("line", 0)
    partner = moved(own, partner_of)

    far = [("line", bit) for bit in range(2, hosts.bit_length() - 1)]
    far += [("centroid", bit) for bit in range(1, columns.bit_length() - 1)]
    by_line, by_column = across("line", 1), across("centroid", 0)
    turned, straight = by_parity(by_line, by_column), by_parity(by_column, by_line)

    distant = moved(centroids, across(*far[-1]))
    level = doubled([centroids], far[:-1])[1:]
    level, partner = lax.optimization_barrier((level, partner))
    near = moved(centroids, straight)
    side = moved(centroids, turned)
    distant, near, side = lax.optimization_barrier((distant, near, side))
    beyond = doubled([distant], far[:-1])[1:]
    packed = pack(line_counts, own, partner, slots, block_rows)
    beyond, packed = lax.optimization_barrier((beyond, packed))
    norms = line_norms(packed, slots)
    near_level = moved(stacked([*level, distant]), straight)
    crossed_level = moved(stacked([near, *level, distant]), turned)
    near_beyond = moved(stacked(beyond), straight)
    crossed_beyond = moved(stacked([near_level, *beyond]), turned)
    corner = moved(near_beyond, turned)

    lines = (packed, partner)
    empty = jnp.full((2 * SUBLANES, own.shape[0]), HUGE_DISTANCE, jnp.float32)
    states = absorb((empty, empty), (centroids, near, side, *level, distant, near_level, *beyond), lines)
    states = absorb(states, (near_beyond, crossed_level), lines)
    mine, theirs = absorb(states, (crossed_beyond,), lines, give=True)
    returned = moved(theirs, partner_of)
    corner, mine, norms = lax.optimization_barrier((corner, mine, norms))
    banks = (corner, moved(corner, partner_of))

    placed = jnp.zeros((2, places, sub_rows), jnp.float32)
    sends = [None, None]
    for parity in (1, 0):
        placed, sends[parity] = last(
            parity,
            placed,
            line_counts,
            destinations,
            packed,
            banks,
            mine,
            returned,
            norms,
            block_rows,
        )
    to_even = moved(sends[1], lambda host, column: (host + 1, column))
    to_odd = moved(sends[0], partner_of)
    return tuple(final(merged(placed, to_even), to_odd))


def solution(mesh):
    in_specs = (P("line", "centroid", None), P("line"), P("line"), P(("centroid", "line"), None))
    out_specs = (P("line", "centroid"), P("line", "centroid"))
    return jax.shard_map(shards, mesh=mesh, in_specs=in_specs, out_specs=out_specs, check_vma=False)
```

```python
import functools

import jax
import jax.numpy as jnp
from jax import lax
from jax.experimental import pallas as pl
from jax.experimental.pallas import tpu as pltpu
from jax.sharding import PartitionSpec as P

HUGE_DISTANCE = 3e38
AXES = ("line", "centroid")
BANK_TILE = 512
LINE_STEP = 1024
SUBLANES = 8
VMEM_LIMIT = 16 * 2**20
VMEM = pl.BlockSpec(memory_space=pltpu.VMEM)
SMEM = pl.BlockSpec(memory_space=pltpu.SMEM)


def moved(value, target):
    hosts, columns = (lax.axis_size(axis) for axis in AXES)
    route = []
    for host in range(hosts):
        for column in range(columns):
            to = target(host, column)
            if to is None:
                continue
            route.append((host * columns + column, to[0] % hosts * columns + to[1]))
    return lax.ppermute(value, AXES, route)


def across(axis, bit):
    if axis == "line":
        return lambda host, column: (host ^ 1 << bit, column)
    return lambda host, column: (host, column ^ 1 << bit)


def by_parity(even, odd):
    return lambda host, column: (odd if host & 1 else even)(host, column)


def call(body, outs, operands, spaces, flops=0, scratch=(), aliases={}, name=None):
    traffic = sum(value.size * value.dtype.itemsize for value in operands)
    return pl.pallas_call(
        body,
        in_specs=list(spaces),
        out_specs=(VMEM,) * len(outs),
        out_shape=outs,
        scratch_shapes=list(scratch),
        input_output_aliases=aliases,
        compiler_params=pltpu.CompilerParams(vmem_limit_bytes=VMEM_LIMIT),
        cost_estimate=pl.CostEstimate(flops=flops, bytes_accessed=traffic, transcendentals=0),
        name=name,
    )(*operands)


def contract(left, right):
    return lax.dot_general(
        left, right, (((1,), (1,)), ((), ())), preferred_element_type=jnp.float32
    )


def fold(first, second, value):
    second = jnp.minimum(second, jnp.maximum(first, value))
    return jnp.minimum(first, value), second


def join(first, second, other_first, other_second):
    runner = jnp.minimum(jnp.minimum(second, other_second), jnp.maximum(first, other_first))
    return jnp.minimum(first, other_first), runner


def pack_kernel(slots, block_rows, count_ref, own_ref, partner_ref, packed_ref):
    lines = own_ref.shape[0]
    per_slot = lines // slots
    half = lines // 2
    packed_ref[:half, :] = own_ref[:half, :]
    for slot in range(slots // 2, slots):
        here = slice(slot * per_slot, (slot + 1) * per_slot)
        other = 3 * slots // 2 - 1 - slot
        theirs = slice(other * per_slot, (other + 1) * per_slot)
        usable = slot * block_rows < count_ref[...]
        packed_ref[here, :] = jnp.where(usable, own_ref[here, :], partner_ref[theirs, :])


def pack(counts, own, partner, slots, block_rows):
    return call(
        functools.partial(pack_kernel, slots, block_rows),
        (jax.ShapeDtypeStruct(own.shape, own.dtype),),
        (counts, own, partner),
        (VMEM, VMEM, VMEM),
        name="pack",
    )[0]


def spread(ref, row, order=None):
    slots, per_slot = ref.shape
    for place in range(slots):
        slot = place if order is None else order[place]
        ref[slot : slot + 1, :] = row[:, place * per_slot : (place + 1) * per_slot]


def norm_kernel(own_ref, norms_ref):
    slots, per_slot = norms_ref.shape
    lines, features = own_ref.shape
    ones = jnp.ones((SUBLANES, features), jnp.bfloat16)
    wide = own_ref[...].astype(jnp.float32)
    square = wide * wide
    high = square.astype(jnp.bfloat16)
    low = (square - high.astype(jnp.float32)).astype(jnp.bfloat16)
    spread(norms_ref, (contract(ones, high) + contract(ones, low))[:1])


def line_norms(own, slots):
    lines, features = own.shape
    out = jax.ShapeDtypeStruct((slots, lines // slots), jnp.float32)
    return call(
        norm_kernel, (out,), (own,), (VMEM,), 32 * SUBLANES * lines * features, name="line_norms"
    )[0]


def prepared(banks):
    scaled = jnp.concatenate([bank * jnp.array(-2, jnp.bfloat16) for bank in banks], axis=0)
    wide = [bank.astype(jnp.float32) for bank in banks]
    norms = [jnp.sum(rows * rows, axis=1, keepdims=True) for rows in wide]
    return scaled, jnp.concatenate(norms, axis=0)


def absorbed(banks, lines, first, second):
    scaled, norms = prepared(banks)
    distance = contract(scaled, lines) + norms
    for row in range(0, distance.shape[0], SUBLANES):
        first, second = fold(first, second, distance[row : row + SUBLANES])
    return first, second


def tiles(bank_refs):
    plan, held, rows = [], [], 0
    for ref in bank_refs:
        tile = min(ref.shape[0], BANK_TILE)
        for at in range(0, ref.shape[0], tile):
            if rows + tile > BANK_TILE:
                plan.append(held)
                held, rows = [], 0
            held.append((ref, at, tile))
            rows += tile
    return plan + [held]


def absorb_kernel(line_count, bank_count, give, *refs):
    line_refs, refs = refs[:line_count], refs[line_count:]
    bank_refs, refs = refs[:bank_count], refs[bank_count:]
    for lines_ref, in_ref, out_ref in zip(line_refs, refs[:line_count], refs[line_count:]):
        lines = lines_ref.shape[0]
        if in_ref is not refs[0]:
            lines //= 2
        step = min(lines, LINE_STEP)
        for at in range(0, lines, step):
            first, second = in_ref[:SUBLANES, at : at + step], in_ref[SUBLANES:, at : at + step]
            for group in tiles(bank_refs):
                banks = [ref[row : row + tile, :] for ref, row, tile in group]
                first, second = absorbed(banks, lines_ref[at : at + step, :], first, second)
            out_ref[:SUBLANES, at : at + step] = first
            out_ref[SUBLANES:, at : at + step] = second
    if give:
        mine_ref, theirs_ref = refs[line_count:]
        half = mine_ref.shape[1] // 2
        theirs_ref[:, half:] = mine_ref[:, half:]


def absorb(states, banks, line_sets, give=False):
    features = banks[0].shape[1]
    rows = sum(bank.shape[0] for bank in banks)
    total = sum(lines.shape[0] for lines in line_sets)
    count = len(line_sets)
    operands = (*line_sets, *banks, *states)
    return call(
        functools.partial(absorb_kernel, count, len(banks), give),
        tuple(jax.ShapeDtypeStruct(state.shape, state.dtype) for state in states),
        operands,
        (VMEM,) * len(operands),
        2 * rows * total * features,
        aliases={count + len(banks) + i: i for i in range(count)},
        name="absorb",
    )


def folded(first, second):
    rows = first.shape[0]
    while rows > 1:
        rows //= 2
        first, second = join(first[:rows], second[:rows], first[rows:], second[rows:])
    return first, second


def last_kernel(parity, block_rows, count_ref, to_ref, lines_ref, *refs):
    bank_refs, refs = refs[:2], refs[2:]
    mine_ref, returned_ref, norms_ref, _, keep_ref, send_ref, slot_ref = refs
    lines, features = lines_ref.shape
    slots, per_slot = norms_ref.shape
    places = keep_ref.shape[1]
    host = lax.axis_index("line")

    @pl.when(lax.rem(host, 2) == parity)
    def work():
        given = folded(returned_ref[:SUBLANES], returned_ref[SUBLANES:])
        order = [*range(slots // 2), *reversed(range(slots // 2, slots))]
        for index, value in enumerate(given):
            spread(slot_ref.at[2 + index], value, order)
        first, second = mine_ref[:SUBLANES], mine_ref[SUBLANES:]
        for group in tiles(bank_refs):
            banks = [ref[row : row + tile, :] for ref, row, tile in group]
            first, second = absorbed(banks, lines_ref[...], first, second)
        for index, value in enumerate(folded(first, second)):
            spread(slot_ref.at[index], value)
        both = join(slot_ref[0], slot_ref[1], slot_ref[2], slot_ref[3])
        both = [(value + norms_ref[...]) / features for value in both]

        following = lax.rem(host + 1, lax.axis_size("line"))
        slot = lax.broadcasted_iota(jnp.int32, (slots, slots), 0)
        across_slots = lax.broadcasted_iota(jnp.int32, (slots, slots), 1)
        to = jnp.where(slot == across_slots, to_ref[...], 0)
        to = jnp.sum(to, axis=1, keepdims=True)
        usable = slot[:, :1] * block_rows < count_ref[...]
        for ref, base in ((keep_ref, host * places), (send_ref, following * places)):
            place = jnp.where(usable, to - base, -1)
            for row in range(places):
                chosen = place == row
                for index, value in enumerate(both):
                    picked = jnp.where(chosen, value, HUGE_DISTANCE)
                    ref[index, row : row + 1, :] = jnp.min(picked, axis=0, keepdims=True)


def last(parity, keep, counts, destinations, own, banks, mine, returned, norms, block_rows):
    lines, features = own.shape
    to = destinations.reshape(1, -1)
    operands = (counts, to, own, *banks, mine, returned, norms, keep)
    placed = jax.ShapeDtypeStruct(keep.shape, keep.dtype)
    return call(
        functools.partial(last_kernel, parity, block_rows),
        (placed, placed),
        operands,
        (VMEM,) * len(operands),
        2 * lines * features * sum(bank.shape[0] for bank in banks),
        scratch=(pltpu.VMEM((4, *norms.shape), jnp.float32),),
        aliases={len(operands) - 1: 0},
        name="last",
    )


def merge_kernel(placed_ref, arrived_ref, out_ref):
    @pl.when(lax.rem(lax.axis_index("line"), 2) == 0)
    def merge():
        out_ref[...] = jnp.minimum(placed_ref[...], arrived_ref[...])


def merged(placed, arrived):
    out = jax.ShapeDtypeStruct(placed.shape, placed.dtype)
    return call(
        merge_kernel, (out,), (placed, arrived), (VMEM,) * 2, 10**9, aliases={0: 0}, name="merged"
    )[0]


def final_kernel(placed_ref, arrived_ref, nearest_ref, runner_ref):
    even = lax.rem(lax.axis_index("line"), 2) == 0
    for index, ref in enumerate((nearest_ref, runner_ref)):

        @pl.when(even)
        def ready(index=index, ref=ref):
            ref[...] = placed_ref[index]

        @pl.when(jnp.logical_not(even))
        def merge(index=index, ref=ref):
            ref[...] = jnp.minimum(placed_ref[index], arrived_ref[index])


def final(placed, arrived):
    out = jax.ShapeDtypeStruct(placed.shape[1:], placed.dtype)
    return call(final_kernel, (out, out), (placed, arrived), (VMEM,) * 2, name="final")


def stacked(pieces):
    return jnp.concatenate(pieces, axis=0) if len(pieces) > 1 else pieces[0]


def doubled(pieces, bits):
    for axis, bit in bits:
        pieces = [*pieces, moved(stacked(pieces), across(axis, bit))]
    return pieces


def shards(line_blocks, line_counts, destinations, centroids):
    hosts, columns = (lax.axis_size(axis) for axis in AXES)
    slots, sub_rows, features = line_blocks.shape
    block_rows = sub_rows * columns
    places = slots // 2
    own = line_blocks.reshape(slots * sub_rows, features)
    partner_of = across("line", 0)
    counts = line_counts.reshape(1, 1)
    partner = moved(own, partner_of)

    far = [("line", bit) for bit in range(2, hosts.bit_length() - 1)]
    far += [("centroid", bit) for bit in range(1, columns.bit_length() - 1)]
    by_line, by_column = across("line", 1), across("centroid", 0)
    turned, straight = by_parity(by_line, by_column), by_parity(by_column, by_line)

    distant = moved(centroids, across(*far[-1]))
    near = moved(centroids, straight)
    level = doubled([centroids], far[:-1])[1:]
    packed = pack(counts, own, partner, slots, block_rows)
    norms = line_norms(packed, slots)
    empty = jnp.full((2 * SUBLANES, own.shape[0]), HUGE_DISTANCE, jnp.float32)
    distant, near, counts = lax.optimization_barrier((distant, near, counts))
    beyond = doubled([distant], far[:-1])[1:]
    level, partner = lax.optimization_barrier((level, partner))
    near_level = moved(stacked([*level, distant]), straight)
    crossed_level = moved(stacked([centroids, near, *level, distant]), turned)
    near_beyond = moved(stacked([*beyond]), straight)
    lines = (packed, partner)
    states = (empty, empty)
    to_turned = stacked([near_level, *beyond])
    crossed_beyond = moved(to_turned, turned)
    near_last = near_beyond
    near_last, norms = lax.optimization_barrier((near_last, norms))
    corner = moved(near_last, turned)
    states = absorb(states, (centroids, near, *level, distant, near_level), lines)
    states = absorb(states, (near_beyond, *beyond, crossed_level), lines)
    mine, theirs = absorb(states, (crossed_beyond,), lines, give=True)
    returned = moved(theirs, partner_of)
    corner, mine, norms = lax.optimization_barrier((corner, mine, norms))
    banks = (corner, moved(corner, partner_of))

    placed = jnp.zeros((2, places, sub_rows), jnp.float32)
    sends = [None, None]
    for parity in (1, 0):
        placed, sends[parity] = last(
            parity,
            placed,
            counts,
            destinations,
            packed,
            banks,
            mine,
            returned,
            norms,
            block_rows,
        )
    to_even = moved(sends[1], lambda host, column: (host + 1, column))
    to_odd = moved(sends[0], partner_of)
    return tuple(final(merged(placed, to_even), to_odd))


def solution(mesh):
    in_specs = (P("line", "centroid", None), P("line"), P("line"), P(("centroid", "line"), None))
    out_specs = (P("line", "centroid"), P("line", "centroid"))
    return jax.shard_map(shards, mesh=mesh, in_specs=in_specs, out_specs=out_specs, check_vma=False)
```

```python
import functools
import math

import jax
import jax.numpy as jnp
from jax import lax
from jax.experimental import pallas as pl
from jax.experimental.pallas import tpu as pltpu
from jax.sharding import PartitionSpec as P

HUGE_DISTANCE = 3e38
AXES = ("line", "centroid")
BANK_TILE = 512
LINE_STEP = 1024
SUBLANES = 8
LANES = 128
VMEM_LIMIT = 16 * 2**20
VMEM = pl.BlockSpec(memory_space=pltpu.VMEM)
SMEM = pl.BlockSpec(memory_space=pltpu.SMEM)


def moved(value, target):
    hosts, columns = (lax.axis_size(axis) for axis in AXES)
    route = []
    for host in range(hosts):
        for column in range(columns):
            to = target(host, column)
            if to is None:
                continue
            route.append((host * columns + column, to[0] % hosts * columns + to[1]))
    return lax.ppermute(value, AXES, route)


def across(axis, bit):
    if axis == "line":
        return lambda host, column: (host ^ 1 << bit, column)
    return lambda host, column: (host, column ^ 1 << bit)


def by_parity(even, odd):
    return lambda host, column: (odd if host & 1 else even)(host, column)


def call(body, outs, operands, spaces, flops=0, scratch=(), aliases={}, name=None):
    traffic = sum(value.size * value.dtype.itemsize for value in operands)
    return pl.pallas_call(
        body,
        in_specs=list(spaces),
        out_specs=(VMEM,) * len(outs),
        out_shape=outs,
        scratch_shapes=list(scratch),
        input_output_aliases=aliases,
        compiler_params=pltpu.CompilerParams(vmem_limit_bytes=VMEM_LIMIT),
        cost_estimate=pl.CostEstimate(flops=flops, bytes_accessed=traffic, transcendentals=0),
        name=name,
    )(*operands)


def contract(left, right):
    return lax.dot_general(
        left, right, (((1,), (1,)), ((), ())), preferred_element_type=jnp.float32
    )


def fold(first, second, value):
    second = jnp.minimum(second, jnp.maximum(first, value))
    return jnp.minimum(first, value), second


def join(first, second, other_first, other_second):
    runner = jnp.minimum(jnp.minimum(second, other_second), jnp.maximum(first, other_first))
    return jnp.minimum(first, other_first), runner


def pack_kernel(slots, block_rows, count_ref, own_ref, partner_ref, packed_ref):
    lines = own_ref.shape[0]
    per_slot = lines // slots
    half = lines // 2
    packed_ref[:half, :] = own_ref[:half, :]
    for slot in range(slots // 2, slots):
        here = slice(slot * per_slot, (slot + 1) * per_slot)
        other = 3 * slots // 2 - 1 - slot
        theirs = slice(other * per_slot, (other + 1) * per_slot)
        usable = slot * block_rows < count_ref[...]
        packed_ref[here, :] = jnp.where(usable, own_ref[here, :], partner_ref[theirs, :])


def pack(counts, own, partner, slots, block_rows):
    return call(
        functools.partial(pack_kernel, slots, block_rows),
        (jax.ShapeDtypeStruct(own.shape, own.dtype),),
        (counts, own, partner),
        (VMEM, VMEM, VMEM),
        name="pack",
    )[0]


def spread(ref, row, order=None):
    slots, per_slot = ref.shape
    for place in range(slots):
        slot = place if order is None else order[place]
        ref[slot : slot + 1, :] = row[:, place * per_slot : (place + 1) * per_slot]


def norm_kernel(own_ref, norms_ref):
    slots, per_slot = norms_ref.shape
    lines, features = own_ref.shape
    lanes = math.gcd(features, LANES)
    wide = own_ref[...].astype(jnp.float32)
    square = wide * wide
    rest = sum(square[:, at : at + lanes] for at in range(0, features, lanes))
    parts = []
    for _ in range(3):
        parts.append(rest.astype(jnp.bfloat16))
        rest = rest - parts[-1].astype(jnp.float32)
    ones = jnp.ones((SUBLANES, 3 * lanes), jnp.bfloat16)
    spread(norms_ref, contract(ones, jnp.concatenate(parts, axis=1))[:1])


def line_norms(own, slots):
    lines, features = own.shape
    out = jax.ShapeDtypeStruct((slots, lines // slots), jnp.float32)
    return call(
        norm_kernel, (out,), (own,), (VMEM,), 32 * SUBLANES * lines * features, name="line_norms"
    )[0]


def prepared(banks):
    scaled = jnp.concatenate([bank * jnp.array(-2, jnp.bfloat16) for bank in banks], axis=0)
    wide = [bank.astype(jnp.float32) for bank in banks]
    norms = [jnp.sum(rows * rows, axis=1, keepdims=True) for rows in wide]
    return scaled, jnp.concatenate(norms, axis=0)


def absorbed(banks, lines, first, second):
    scaled, norms = prepared(banks)
    distance = contract(scaled, lines) + norms
    rows = distance.shape[0]
    for row in range(0, rows, 2 * SUBLANES):
        low, high = distance[row : row + SUBLANES], distance[row + SUBLANES : row + 2 * SUBLANES]
        first, second = join(first, second, jnp.minimum(low, high), jnp.maximum(low, high))
    return first, second


def tiles(bank_refs):
    plan, held, rows = [], [], 0
    for ref in bank_refs:
        tile = min(ref.shape[0], BANK_TILE)
        for at in range(0, ref.shape[0], tile):
            if rows + tile > BANK_TILE:
                plan.append(held)
                held, rows = [], 0
            held.append((ref, at, tile))
            rows += tile
    return plan + [held]


def absorb_kernel(line_count, bank_count, give, *refs):
    line_refs, refs = refs[:line_count], refs[line_count:]
    bank_refs, refs = refs[:bank_count], refs[bank_count:]
    for lines_ref, in_ref, out_ref in zip(line_refs, refs[:line_count], refs[line_count:]):
        lines = lines_ref.shape[0]
        if in_ref is not refs[0]:
            lines //= 2
        step = min(lines, LINE_STEP)
        for at in range(0, lines, step):
            first, second = in_ref[:SUBLANES, at : at + step], in_ref[SUBLANES:, at : at + step]
            for group in tiles(bank_refs):
                banks = [ref[row : row + tile, :] for ref, row, tile in group]
                first, second = absorbed(banks, lines_ref[at : at + step, :], first, second)
            out_ref[:SUBLANES, at : at + step] = first
            out_ref[SUBLANES:, at : at + step] = second
    if give:
        mine_ref, theirs_ref = refs[line_count:]
        half = mine_ref.shape[1] // 2
        theirs_ref[:, half:] = mine_ref[:, half:]


def absorb(states, banks, line_sets, give=False):
    features = banks[0].shape[1]
    rows = sum(bank.shape[0] for bank in banks)
    total = sum(lines.shape[0] for lines in line_sets)
    count = len(line_sets)
    operands = (*line_sets, *banks, *states)
    return call(
        functools.partial(absorb_kernel, count, len(banks), give),
        tuple(jax.ShapeDtypeStruct(state.shape, state.dtype) for state in states),
        operands,
        (VMEM,) * len(operands),
        2 * rows * total * features,
        aliases={count + len(banks) + i: i for i in range(count)},
        name="absorb",
    )


def folded(first, second):
    rows = first.shape[0]
    while rows > 1:
        rows //= 2
        first, second = join(first[:rows], second[:rows], first[rows:], second[rows:])
    return first, second


def last_kernel(parity, block_rows, count_ref, to_ref, lines_ref, *refs):
    bank_refs, refs = refs[:2], refs[2:]
    mine_ref, returned_ref, norms_ref, _, keep_ref, send_ref, slot_ref = refs
    lines, features = lines_ref.shape
    slots, per_slot = norms_ref.shape
    places = keep_ref.shape[1]
    host = lax.axis_index("line")

    @pl.when(lax.rem(host, 2) == parity)
    def work():
        given = folded(returned_ref[:SUBLANES], returned_ref[SUBLANES:])
        order = [*range(slots // 2), *reversed(range(slots // 2, slots))]
        for index, value in enumerate(given):
            spread(slot_ref.at[2 + index], value, order)
        first, second = mine_ref[:SUBLANES], mine_ref[SUBLANES:]
        for group in tiles(bank_refs):
            banks = [ref[row : row + tile, :] for ref, row, tile in group]
            first, second = absorbed(banks, lines_ref[...], first, second)
        for index, value in enumerate(folded(first, second)):
            spread(slot_ref.at[index], value)
        both = join(slot_ref[0], slot_ref[1], slot_ref[2], slot_ref[3])
        both = [(value + norms_ref[...]) / features for value in both]

        following = lax.rem(host + 1, lax.axis_size("line"))
        slot = lax.broadcasted_iota(jnp.int32, (slots, slots), 0)
        across_slots = lax.broadcasted_iota(jnp.int32, (slots, slots), 1)
        to = jnp.where(slot == across_slots, to_ref[...], 0)
        to = jnp.sum(to, axis=1, keepdims=True)
        usable = slot[:, :1] * block_rows < count_ref[...]
        for ref, base in ((keep_ref, host * places), (send_ref, following * places)):
            place = jnp.where(usable, to - base, -1)
            for row in range(places):
                chosen = place == row
                for index, value in enumerate(both):
                    picked = jnp.where(chosen, value, HUGE_DISTANCE)
                    ref[index, row : row + 1, :] = jnp.min(picked, axis=0, keepdims=True)


def last(parity, keep, counts, destinations, own, banks, mine, returned, norms, block_rows):
    lines, features = own.shape
    to = destinations.reshape(1, -1)
    operands = (counts, to, own, *banks, mine, returned, norms, keep)
    placed = jax.ShapeDtypeStruct(keep.shape, keep.dtype)
    return call(
        functools.partial(last_kernel, parity, block_rows),
        (placed, placed),
        operands,
        (VMEM,) * len(operands),
        2 * lines * features * sum(bank.shape[0] for bank in banks),
        scratch=(pltpu.VMEM((4, *norms.shape), jnp.float32),),
        aliases={len(operands) - 1: 0},
        name="last",
    )


def merge_kernel(placed_ref, arrived_ref, out_ref):
    @pl.when(lax.rem(lax.axis_index("line"), 2) == 0)
    def merge():
        out_ref[...] = jnp.minimum(placed_ref[...], arrived_ref[...])


def merged(placed, arrived):
    out = jax.ShapeDtypeStruct(placed.shape, placed.dtype)
    return call(
        merge_kernel, (out,), (placed, arrived), (VMEM,) * 2, 10**9, aliases={0: 0}, name="merged"
    )[0]


def final_kernel(placed_ref, arrived_ref, nearest_ref, runner_ref):
    even = lax.rem(lax.axis_index("line"), 2) == 0
    for index, ref in enumerate((nearest_ref, runner_ref)):

        @pl.when(even)
        def ready(index=index, ref=ref):
            ref[...] = placed_ref[index]

        @pl.when(jnp.logical_not(even))
        def merge(index=index, ref=ref):
            ref[...] = jnp.minimum(placed_ref[index], arrived_ref[index])


def final(placed, arrived):
    out = jax.ShapeDtypeStruct(placed.shape[1:], placed.dtype)
    return call(final_kernel, (out, out), (placed, arrived), (VMEM,) * 2, name="final")


def stacked(pieces):
    return jnp.concatenate(pieces, axis=0) if len(pieces) > 1 else pieces[0]


def doubled(pieces, bits):
    for axis, bit in bits:
        pieces = [*pieces, moved(stacked(pieces), across(axis, bit))]
    return pieces


def shards(line_blocks, line_counts, destinations, centroids):
    hosts, columns = (lax.axis_size(axis) for axis in AXES)
    slots, sub_rows, features = line_blocks.shape
    block_rows = sub_rows * columns
    places = slots // 2
    own = line_blocks.reshape(slots * sub_rows, features)
    partner_of = across("line", 0)
    counts = line_counts.reshape(1, 1)
    partner = moved(own, partner_of)

    far = [("line", bit) for bit in range(2, hosts.bit_length() - 1)]
    far += [("centroid", bit) for bit in range(1, columns.bit_length() - 1)]
    by_line, by_column = across("line", 1), across("centroid", 0)
    turned, straight = by_parity(by_line, by_column), by_parity(by_column, by_line)

    distant = moved(centroids, across(*far[-1]))
    near = moved(centroids, straight)
    level = doubled([centroids], far[:-1])[1:]
    packed = pack(counts, own, partner, slots, block_rows)
    norms = line_norms(packed, slots)
    empty = jnp.full((2 * SUBLANES, own.shape[0]), HUGE_DISTANCE, jnp.float32)
    distant, counts = lax.optimization_barrier((distant, counts))
    beyond = doubled([distant], far[:-1])[1:]
    level, partner = lax.optimization_barrier((level, partner))
    near_level = moved(stacked([*level, distant]), straight)
    crossed_level = moved(stacked([centroids, near, *level, distant]), turned)
    near_beyond = moved(stacked([*beyond]), straight)
    lines = (packed, partner)
    states = (empty, empty)
    to_turned = stacked([near_level, *beyond])
    crossed_beyond = moved(to_turned, turned)
    near_last = near_beyond
    near_last, norms = lax.optimization_barrier((near_last, norms))
    corner = moved(near_last, turned)
    states = absorb(states, (centroids, near, *level, distant, near_level), lines)
    states = absorb(states, (near_beyond, *beyond, crossed_level), lines)
    mine, theirs = absorb(states, (crossed_beyond,), lines, give=True)
    returned = moved(theirs, partner_of)
    corner, mine, norms = lax.optimization_barrier((corner, mine, norms))
    banks = (corner, moved(corner, partner_of))

    placed = jnp.zeros((2, places, sub_rows), jnp.float32)
    sends = [None, None]
    for parity in (1, 0):
        placed, sends[parity] = last(
            parity,
            placed,
            counts,
            destinations,
            packed,
            banks,
            mine,
            returned,
            norms,
            block_rows,
        )
    to_even = moved(sends[1], lambda host, column: (host + 1, column))
    to_odd = moved(sends[0], partner_of)
    return tuple(final(merged(placed, to_even), to_odd))


def solution(mesh):
    in_specs = (P("line", "centroid", None), P("line"), P("line"), P(("centroid", "line"), None))
    out_specs = (P("line", "centroid"), P("line", "centroid"))
    return jax.shard_map(shards, mesh=mesh, in_specs=in_specs, out_specs=out_specs, check_vma=False)
```

```python
import functools
import math

import jax
import jax.numpy as jnp
from jax import lax
from jax.experimental import pallas as pl
from jax.experimental.pallas import tpu as pltpu
from jax.sharding import PartitionSpec as P

HUGE_DISTANCE = 3e38
AXES = ("line", "centroid")
BANK_TILE = 512
LINE_STEP = 1024
SUBLANES = 8
LANES = 128
VMEM_LIMIT = 16 * 2**20
VMEM = pl.BlockSpec(memory_space=pltpu.VMEM)
SMEM = pl.BlockSpec(memory_space=pltpu.SMEM)


def moved(value, target):
    hosts, columns = (lax.axis_size(axis) for axis in AXES)
    route = []
    for host in range(hosts):
        for column in range(columns):
            to = target(host, column)
            if to is None:
                continue
            route.append((host * columns + column, to[0] % hosts * columns + to[1]))
    return lax.ppermute(value, AXES, route)


def across(axis, bit):
    if axis == "line":
        return lambda host, column: (host ^ 1 << bit, column)
    return lambda host, column: (host, column ^ 1 << bit)


def by_parity(even, odd):
    return lambda host, column: (odd if host & 1 else even)(host, column)


def call(body, outs, operands, spaces, flops=0, scratch=(), aliases={}, name=None):
    traffic = sum(value.size * value.dtype.itemsize for value in operands)
    return pl.pallas_call(
        body,
        in_specs=list(spaces),
        out_specs=(VMEM,) * len(outs),
        out_shape=outs,
        scratch_shapes=list(scratch),
        input_output_aliases=aliases,
        compiler_params=pltpu.CompilerParams(vmem_limit_bytes=VMEM_LIMIT),
        cost_estimate=pl.CostEstimate(flops=flops, bytes_accessed=traffic, transcendentals=0),
        name=name,
    )(*operands)


def contract(left, right):
    return lax.dot_general(
        left, right, (((1,), (1,)), ((), ())), preferred_element_type=jnp.float32
    )


def fold(first, second, value):
    second = jnp.minimum(second, jnp.maximum(first, value))
    return jnp.minimum(first, value), second


def join(first, second, other_first, other_second):
    runner = jnp.minimum(jnp.minimum(second, other_second), jnp.maximum(first, other_first))
    return jnp.minimum(first, other_first), runner


def pack_kernel(slots, block_rows, count_ref, own_ref, partner_ref, packed_ref):
    lines = own_ref.shape[0]
    per_slot = lines // slots
    half = lines // 2
    packed_ref[:half, :] = own_ref[:half, :]
    for slot in range(slots // 2, slots):
        here = slice(slot * per_slot, (slot + 1) * per_slot)
        other = 3 * slots // 2 - 1 - slot
        theirs = slice(other * per_slot, (other + 1) * per_slot)
        usable = slot * block_rows < count_ref[...]
        packed_ref[here, :] = jnp.where(usable, own_ref[here, :], partner_ref[theirs, :])


def pack(counts, own, partner, slots, block_rows):
    return call(
        functools.partial(pack_kernel, slots, block_rows),
        (jax.ShapeDtypeStruct(own.shape, own.dtype),),
        (counts, own, partner),
        (VMEM, VMEM, VMEM),
        name="pack",
    )[0]


def spread(ref, row, order=None):
    slots, per_slot = ref.shape
    for place in range(slots):
        slot = place if order is None else order[place]
        ref[slot : slot + 1, :] = row[:, place * per_slot : (place + 1) * per_slot]


def norm_kernel(own_ref, norms_ref):
    slots, per_slot = norms_ref.shape
    lines, features = own_ref.shape
    lanes = math.gcd(features, LANES)
    wide = own_ref[...].astype(jnp.float32)
    square = wide * wide
    rest = sum(square[:, at : at + lanes] for at in range(0, features, lanes))
    parts = []
    for _ in range(3):
        parts.append(rest.astype(jnp.bfloat16))
        rest = rest - parts[-1].astype(jnp.float32)
    ones = jnp.ones((SUBLANES, 3 * lanes), jnp.bfloat16)
    spread(norms_ref, contract(ones, jnp.concatenate(parts, axis=1))[:1])


def line_norms(own, slots):
    lines, features = own.shape
    out = jax.ShapeDtypeStruct((slots, lines // slots), jnp.float32)
    return call(
        norm_kernel, (out,), (own,), (VMEM,), 32 * SUBLANES * lines * features, name="line_norms"
    )[0]


def prepared(banks):
    scaled = jnp.concatenate([bank * jnp.array(-2, jnp.bfloat16) for bank in banks], axis=0)
    wide = [bank.astype(jnp.float32) for bank in banks]
    norms = [jnp.sum(rows * rows, axis=1, keepdims=True) for rows in wide]
    return scaled, jnp.concatenate(norms, axis=0)


def absorbed(banks, lines, first, second):
    scaled, norms = prepared(banks)
    distance = contract(scaled, lines) + norms
    rows = distance.shape[0]
    for row in range(0, rows, 2 * SUBLANES):
        low, high = distance[row : row + SUBLANES], distance[row + SUBLANES : row + 2 * SUBLANES]
        first, second = join(first, second, jnp.minimum(low, high), jnp.maximum(low, high))
    return first, second


def tiles(bank_refs):
    plan, held, rows = [], [], 0
    for ref in bank_refs:
        tile = min(ref.shape[0], BANK_TILE)
        for at in range(0, ref.shape[0], tile):
            if rows + tile > BANK_TILE:
                plan.append(held)
                held, rows = [], 0
            held.append((ref, at, tile))
            rows += tile
    return plan + [held]


def absorb_kernel(line_count, bank_count, give, *refs):
    line_refs, refs = refs[:line_count], refs[line_count:]
    bank_refs, refs = refs[:bank_count], refs[bank_count:]
    for lines_ref, in_ref, out_ref in zip(line_refs, refs[:line_count], refs[line_count:]):
        lines = lines_ref.shape[0]
        if in_ref is not refs[0]:
            lines //= 2
        step = min(lines, LINE_STEP)
        for at in range(0, lines, step):
            first, second = in_ref[:SUBLANES, at : at + step], in_ref[SUBLANES:, at : at + step]
            for group in tiles(bank_refs):
                banks = [ref[row : row + tile, :] for ref, row, tile in group]
                first, second = absorbed(banks, lines_ref[at : at + step, :], first, second)
            out_ref[:SUBLANES, at : at + step] = first
            out_ref[SUBLANES:, at : at + step] = second
    if give:
        mine_ref, theirs_ref, given_ref = refs[line_count:]
        half = mine_ref.shape[1] // 2
        both = jnp.concatenate([theirs_ref[:, :half], mine_ref[:, half:]], axis=1)
        first, second = both[:SUBLANES], both[SUBLANES:]
        rows = SUBLANES // 2
        first, second = join(first[:rows], second[:rows], first[rows:], second[rows:])
        given_ref[:rows] = first
        given_ref[rows:] = second


def absorb(states, banks, line_sets, give=False):
    features = banks[0].shape[1]
    rows = sum(bank.shape[0] for bank in banks)
    total = sum(lines.shape[0] for lines in line_sets)
    count = len(line_sets)
    operands = (*line_sets, *banks, *states)
    outs = tuple(jax.ShapeDtypeStruct(state.shape, state.dtype) for state in states)
    if give:
        outs += (jax.ShapeDtypeStruct((SUBLANES, states[0].shape[1]), states[0].dtype),)
    return call(
        functools.partial(absorb_kernel, count, len(banks), give),
        outs,
        operands,
        (VMEM,) * len(operands),
        2 * rows * total * features,
        aliases={count + len(banks) + i: i for i in range(count)},
        name="absorb",
    )


def folded(first, second):
    rows = first.shape[0]
    while rows > 1:
        rows //= 2
        first, second = join(first[:rows], second[:rows], first[rows:], second[rows:])
    return first, second


def last_kernel(parity, block_rows, count_ref, to_ref, lines_ref, *refs):
    bank_refs, refs = refs[:2], refs[2:]
    mine_ref, returned_ref, norms_ref, _, keep_ref, send_ref, slot_ref = refs
    lines, features = lines_ref.shape
    slots, per_slot = norms_ref.shape
    places = keep_ref.shape[1]
    host = lax.axis_index("line")

    @pl.when(lax.rem(host, 2) == parity)
    def work():
        rows = SUBLANES // 2
        given = folded(returned_ref[:rows], returned_ref[rows:])
        order = [*range(slots // 2), *reversed(range(slots // 2, slots))]
        for index, value in enumerate(given):
            spread(slot_ref.at[2 + index], value, order)
        first, second = mine_ref[:SUBLANES], mine_ref[SUBLANES:]
        for group in tiles(bank_refs):
            banks = [ref[row : row + tile, :] for ref, row, tile in group]
            first, second = absorbed(banks, lines_ref[...], first, second)
        for index, value in enumerate(folded(first, second)):
            spread(slot_ref.at[index], value)
        both = join(slot_ref[0], slot_ref[1], slot_ref[2], slot_ref[3])
        both = [(value + norms_ref[...]) / features for value in both]

        following = lax.rem(host + 1, lax.axis_size("line"))
        slot = lax.broadcasted_iota(jnp.int32, (slots, slots), 0)
        across_slots = lax.broadcasted_iota(jnp.int32, (slots, slots), 1)
        to = jnp.where(slot == across_slots, to_ref[...], 0)
        to = jnp.sum(to, axis=1, keepdims=True)
        usable = slot[:, :1] * block_rows < count_ref[...]
        for ref, base in ((keep_ref, host * places), (send_ref, following * places)):
            place = jnp.where(usable, to - base, -1)
            for row in range(places):
                chosen = place == row
                for index, value in enumerate(both):
                    picked = jnp.where(chosen, value, HUGE_DISTANCE)
                    ref[index, row : row + 1, :] = jnp.min(picked, axis=0, keepdims=True)


def last(parity, keep, counts, destinations, own, banks, mine, returned, norms, block_rows):
    lines, features = own.shape
    to = destinations.reshape(1, -1)
    operands = (counts, to, own, *banks, mine, returned, norms, keep)
    placed = jax.ShapeDtypeStruct(keep.shape, keep.dtype)
    return call(
        functools.partial(last_kernel, parity, block_rows),
        (placed, placed),
        operands,
        (VMEM,) * len(operands),
        2 * lines * features * sum(bank.shape[0] for bank in banks),
        scratch=(pltpu.VMEM((4, *norms.shape), jnp.float32),),
        aliases={len(operands) - 1: 0},
        name="last",
    )


def merge_kernel(placed_ref, arrived_ref, out_ref):
    @pl.when(lax.rem(lax.axis_index("line"), 2) == 0)
    def merge():
        out_ref[...] = jnp.minimum(placed_ref[...], arrived_ref[...])


def merged(placed, arrived):
    out = jax.ShapeDtypeStruct(placed.shape, placed.dtype)
    return call(
        merge_kernel, (out,), (placed, arrived), (VMEM,) * 2, 10**9, aliases={0: 0}, name="merged"
    )[0]


def final_kernel(placed_ref, arrived_ref, nearest_ref, runner_ref):
    even = lax.rem(lax.axis_index("line"), 2) == 0
    for index, ref in enumerate((nearest_ref, runner_ref)):

        @pl.when(even)
        def ready(index=index, ref=ref):
            ref[...] = placed_ref[index]

        @pl.when(jnp.logical_not(even))
        def merge(index=index, ref=ref):
            ref[...] = jnp.minimum(placed_ref[index], arrived_ref[index])


def final(placed, arrived):
    out = jax.ShapeDtypeStruct(placed.shape[1:], placed.dtype)
    return call(final_kernel, (out, out), (placed, arrived), (VMEM,) * 2, name="final")


def stacked(pieces):
    return jnp.concatenate(pieces, axis=0) if len(pieces) > 1 else pieces[0]


def doubled(pieces, bits):
    for axis, bit in bits:
        pieces = [*pieces, moved(stacked(pieces), across(axis, bit))]
    return pieces


def shards(line_blocks, line_counts, destinations, centroids):
    hosts, columns = (lax.axis_size(axis) for axis in AXES)
    slots, sub_rows, features = line_blocks.shape
    block_rows = sub_rows * columns
    places = slots // 2
    own = line_blocks.reshape(slots * sub_rows, features)
    partner_of = across("line", 0)
    counts = line_counts.reshape(1, 1)
    partner = moved(own, partner_of)

    far = [("line", bit) for bit in range(2, hosts.bit_length() - 1)]
    far += [("centroid", bit) for bit in range(1, columns.bit_length() - 1)]
    by_line, by_column = across("line", 1), across("centroid", 0)
    turned, straight = by_parity(by_line, by_column), by_parity(by_column, by_line)

    distant = moved(centroids, across(*far[-1]))
    near = moved(centroids, straight)
    level = doubled([centroids], far[:-1])[1:]
    packed = pack(counts, own, partner, slots, block_rows)
    norms = line_norms(packed, slots)
    empty = jnp.full((2 * SUBLANES, own.shape[0]), HUGE_DISTANCE, jnp.float32)
    distant, counts = lax.optimization_barrier((distant, counts))
    beyond = doubled([distant], far[:-1])[1:]
    level, partner = lax.optimization_barrier((level, partner))
    near_level = moved(stacked([*level, distant]), straight)
    crossed_level = moved(stacked([centroids, near, *level, distant]), turned)
    near_beyond = moved(stacked([*beyond]), straight)
    lines = (packed, partner)
    states = (empty, empty)
    to_turned = stacked([near_level, *beyond])
    crossed_beyond = moved(to_turned, turned)
    near_last = near_beyond
    near_last, norms = lax.optimization_barrier((near_last, norms))
    corner = moved(near_last, turned)
    states = absorb(states, (centroids, near, *level, distant, near_level), lines)
    states = absorb(states, (near_beyond, *beyond, crossed_level), lines)
    mine, _, given = absorb(states, (crossed_beyond,), lines, give=True)
    returned = moved(given, partner_of)
    corner, mine, norms = lax.optimization_barrier((corner, mine, norms))
    banks = (corner, moved(corner, partner_of))

    placed = jnp.zeros((2, places, sub_rows), jnp.float32)
    sends = [None, None]
    for parity in (1, 0):
        placed, sends[parity] = last(
            parity,
            placed,
            counts,
            destinations,
            packed,
            banks,
            mine,
            returned,
            norms,
            block_rows,
        )
    to_even = moved(sends[1], lambda host, column: (host + 1, column))
    to_odd = moved(sends[0], partner_of)
    return tuple(final(merged(placed, to_even), to_odd))


def solution(mesh):
    in_specs = (P("line", "centroid", None), P("line"), P("line"), P(("centroid", "line"), None))
    out_specs = (P("line", "centroid"), P("line", "centroid"))
    return jax.shard_map(shards, mesh=mesh, in_specs=in_specs, out_specs=out_specs, check_vma=False)
```

```python
import functools
import math

import jax
import jax.numpy as jnp
from jax import lax
from jax.experimental import pallas as pl
from jax.experimental.pallas import tpu as pltpu
from jax.sharding import PartitionSpec as P

HUGE_DISTANCE = 3e38
AXES = ("line", "centroid")
BANK_TILE = 512
LINE_STEP = 1024
SUBLANES = 8
LANES = 128
VMEM_LIMIT = 16 * 2**20
VMEM = pl.BlockSpec(memory_space=pltpu.VMEM)
SMEM = pl.BlockSpec(memory_space=pltpu.SMEM)


def moved(value, target):
    hosts, columns = (lax.axis_size(axis) for axis in AXES)
    route = []
    for host in range(hosts):
        for column in range(columns):
            to = target(host, column)
            if to is None:
                continue
            route.append((host * columns + column, to[0] % hosts * columns + to[1]))
    return lax.ppermute(value, AXES, route)


def across(axis, bit):
    if axis == "line":
        return lambda host, column: (host ^ 1 << bit, column)
    return lambda host, column: (host, column ^ 1 << bit)


def by_parity(even, odd):
    return lambda host, column: (odd if host & 1 else even)(host, column)


def call(body, outs, operands, spaces, flops=0, scratch=(), aliases={}, name=None):
    traffic = sum(value.size * value.dtype.itemsize for value in operands)
    return pl.pallas_call(
        body,
        in_specs=list(spaces),
        out_specs=(VMEM,) * len(outs),
        out_shape=outs,
        scratch_shapes=list(scratch),
        input_output_aliases=aliases,
        compiler_params=pltpu.CompilerParams(vmem_limit_bytes=VMEM_LIMIT),
        cost_estimate=pl.CostEstimate(flops=flops, bytes_accessed=traffic, transcendentals=0),
        name=name,
    )(*operands)


def contract(left, right):
    return lax.dot_general(
        left, right, (((1,), (1,)), ((), ())), preferred_element_type=jnp.float32
    )


def fold(first, second, value):
    second = jnp.minimum(second, jnp.maximum(first, value))
    return jnp.minimum(first, value), second


def join(first, second, other_first, other_second):
    runner = jnp.minimum(jnp.minimum(second, other_second), jnp.maximum(first, other_first))
    return jnp.minimum(first, other_first), runner


def pack_kernel(slots, block_rows, count_ref, own_ref, partner_ref, packed_ref):
    lines = own_ref.shape[0]
    per_slot = lines // slots
    half = lines // 2
    packed_ref[:half, :] = own_ref[:half, :]
    for slot in range(slots // 2, slots):
        here = slice(slot * per_slot, (slot + 1) * per_slot)
        other = 3 * slots // 2 - 1 - slot
        theirs = slice(other * per_slot, (other + 1) * per_slot)
        usable = slot * block_rows < count_ref[...]
        packed_ref[here, :] = jnp.where(usable, own_ref[here, :], partner_ref[theirs, :])


def pack(counts, own, partner, slots, block_rows):
    return call(
        functools.partial(pack_kernel, slots, block_rows),
        (jax.ShapeDtypeStruct(own.shape, own.dtype),),
        (counts, own, partner),
        (VMEM, VMEM, VMEM),
        name="pack",
    )[0]


def spread(ref, row, order=None):
    slots, per_slot = ref.shape
    for place in range(slots):
        slot = place if order is None else order[place]
        ref[slot : slot + 1, :] = row[:, place * per_slot : (place + 1) * per_slot]


def norm_kernel(own_ref, norms_ref):
    slots, per_slot = norms_ref.shape
    lines, features = own_ref.shape
    lanes = math.gcd(features, LANES)
    wide = own_ref[...].astype(jnp.float32)
    square = wide * wide
    rest = sum(square[:, at : at + lanes] for at in range(0, features, lanes))
    parts = []
    for _ in range(3):
        parts.append(rest.astype(jnp.bfloat16))
        rest = rest - parts[-1].astype(jnp.float32)
    ones = jnp.ones((SUBLANES, 3 * lanes), jnp.bfloat16)
    spread(norms_ref, contract(ones, jnp.concatenate(parts, axis=1))[:1])


def line_norms(own, slots):
    lines, features = own.shape
    out = jax.ShapeDtypeStruct((slots, lines // slots), jnp.float32)
    return call(
        norm_kernel, (out,), (own,), (VMEM,), 32 * SUBLANES * lines * features, name="line_norms"
    )[0]


def prepared(banks):
    scaled = jnp.concatenate([bank * jnp.array(-2, jnp.bfloat16) for bank in banks], axis=0)
    wide = [bank.astype(jnp.float32) for bank in banks]
    norms = [jnp.sum(rows * rows, axis=1, keepdims=True) for rows in wide]
    return scaled, jnp.concatenate(norms, axis=0)


def absorbed(banks, lines, first, second):
    scaled, norms = prepared(banks)
    distance = contract(scaled, lines) + norms
    rows = distance.shape[0]
    for row in range(0, rows, 2 * SUBLANES):
        low, high = distance[row : row + SUBLANES], distance[row + SUBLANES : row + 2 * SUBLANES]
        first, second = join(first, second, jnp.minimum(low, high), jnp.maximum(low, high))
    return first, second


def tiles(bank_refs):
    plan, held, rows = [], [], 0
    for ref in bank_refs:
        tile = min(ref.shape[0], BANK_TILE)
        for at in range(0, ref.shape[0], tile):
            if rows + tile > BANK_TILE:
                plan.append(held)
                held, rows = [], 0
            held.append((ref, at, tile))
            rows += tile
    return plan + [held]


def absorb_kernel(line_count, bank_count, give, *refs):
    line_refs, refs = refs[:line_count], refs[line_count:]
    bank_refs, refs = refs[:bank_count], refs[bank_count:]
    for lines_ref, in_ref, out_ref in zip(line_refs, refs[:line_count], refs[line_count:]):
        lines = lines_ref.shape[0]
        if in_ref is not refs[0]:
            lines //= 2
        step = min(lines, LINE_STEP)
        for at in range(0, lines, step):
            first, second = in_ref[:SUBLANES, at : at + step], in_ref[SUBLANES:, at : at + step]
            for group in tiles(bank_refs):
                banks = [ref[row : row + tile, :] for ref, row, tile in group]
                first, second = absorbed(banks, lines_ref[at : at + step, :], first, second)
            out_ref[:SUBLANES, at : at + step] = first
            out_ref[SUBLANES:, at : at + step] = second
    if give:
        mine_ref, theirs_ref = refs[line_count:]
        half = mine_ref.shape[1] // 2
        theirs_ref[:, half:] = mine_ref[:, half:]


def absorb(states, banks, line_sets, give=False):
    features = banks[0].shape[1]
    rows = sum(bank.shape[0] for bank in banks)
    total = sum(lines.shape[0] for lines in line_sets)
    count = len(line_sets)
    operands = (*line_sets, *banks, *states)
    return call(
        functools.partial(absorb_kernel, count, len(banks), give),
        tuple(jax.ShapeDtypeStruct(state.shape, state.dtype) for state in states),
        operands,
        (VMEM,) * len(operands),
        2 * rows * total * features,
        aliases={count + len(banks) + i: i for i in range(count)},
        name="absorb",
    )


def folded(first, second):
    rows = first.shape[0]
    while rows > 1:
        rows //= 2
        first, second = join(first[:rows], second[:rows], first[rows:], second[rows:])
    return first, second


def last_kernel(parity, block_rows, count_ref, to_ref, lines_ref, *refs):
    bank_refs, refs = refs[:2], refs[2:]
    mine_ref, returned_ref, norms_ref, _, keep_ref, send_ref, slot_ref = refs
    lines, features = lines_ref.shape
    slots, per_slot = norms_ref.shape
    places = keep_ref.shape[1]
    host = lax.axis_index("line")

    @pl.when(lax.rem(host, 2) == parity)
    def work():
        given = folded(returned_ref[:SUBLANES], returned_ref[SUBLANES:])
        order = [*range(slots // 2), *reversed(range(slots // 2, slots))]
        for index, value in enumerate(given):
            spread(slot_ref.at[2 + index], value, order)
        first, second = mine_ref[:SUBLANES], mine_ref[SUBLANES:]
        for group in tiles(bank_refs):
            banks = [ref[row : row + tile, :] for ref, row, tile in group]
            first, second = absorbed(banks, lines_ref[...], first, second)
        for index, value in enumerate(folded(first, second)):
            spread(slot_ref.at[index], value)
        both = join(slot_ref[0], slot_ref[1], slot_ref[2], slot_ref[3])
        both = [(value + norms_ref[...]) / features for value in both]

        following = lax.rem(host + 1, lax.axis_size("line"))
        slot = lax.broadcasted_iota(jnp.int32, (slots, slots), 0)
        across_slots = lax.broadcasted_iota(jnp.int32, (slots, slots), 1)
        to = jnp.where(slot == across_slots, to_ref[...], 0)
        to = jnp.sum(to, axis=1, keepdims=True)
        usable = slot[:, :1] * block_rows < count_ref[...]
        for ref, base in ((keep_ref, host * places), (send_ref, following * places)):
            place = jnp.where(usable, to - base, -1)
            for row in range(places):
                chosen = place == row
                for index, value in enumerate(both):
                    picked = jnp.where(chosen, value, HUGE_DISTANCE)
                    ref[index, row : row + 1, :] = jnp.min(picked, axis=0, keepdims=True)


def last(parity, keep, counts, destinations, own, banks, mine, returned, norms, block_rows):
    lines, features = own.shape
    to = destinations.reshape(1, -1)
    operands = (counts, to, own, *banks, mine, returned, norms, keep)
    placed = jax.ShapeDtypeStruct(keep.shape, keep.dtype)
    return call(
        functools.partial(last_kernel, parity, block_rows),
        (placed, placed),
        operands,
        (VMEM,) * len(operands),
        2 * lines * features * sum(bank.shape[0] for bank in banks),
        scratch=(pltpu.VMEM((4, *norms.shape), jnp.float32),),
        aliases={len(operands) - 1: 0},
        name="last",
    )


def merge_kernel(placed_ref, arrived_ref, out_ref):
    @pl.when(lax.rem(lax.axis_index("line"), 2) == 0)
    def merge():
        out_ref[...] = jnp.minimum(placed_ref[...], arrived_ref[...])


def merged(placed, arrived):
    out = jax.ShapeDtypeStruct(placed.shape, placed.dtype)
    return call(
        merge_kernel, (out,), (placed, arrived), (VMEM,) * 2, 10**9, aliases={0: 0}, name="merged"
    )[0]


def final_kernel(placed_ref, arrived_ref, nearest_ref, runner_ref):
    even = lax.rem(lax.axis_index("line"), 2) == 0
    for index, ref in enumerate((nearest_ref, runner_ref)):

        @pl.when(even)
        def ready(index=index, ref=ref):
            ref[...] = placed_ref[index]

        @pl.when(jnp.logical_not(even))
        def merge(index=index, ref=ref):
            ref[...] = jnp.minimum(placed_ref[index], arrived_ref[index])


def final(placed, arrived):
    out = jax.ShapeDtypeStruct(placed.shape[1:], placed.dtype)
    return call(final_kernel, (out, out), (placed, arrived), (VMEM,) * 2, name="final")


def stacked(pieces):
    return jnp.concatenate(pieces, axis=0) if len(pieces) > 1 else pieces[0]


def doubled(pieces, bits):
    for axis, bit in bits:
        pieces = [*pieces, moved(stacked(pieces), across(axis, bit))]
    return pieces


def shards(line_blocks, line_counts, destinations, centroids):
    hosts, columns = (lax.axis_size(axis) for axis in AXES)
    slots, sub_rows, features = line_blocks.shape
    block_rows = sub_rows * columns
    places = slots // 2
    own = line_blocks.reshape(slots * sub_rows, features)
    partner_of = across("line", 0)
    counts = line_counts.reshape(1, 1)
    partner = moved(own, partner_of)

    far = [("line", bit) for bit in range(2, hosts.bit_length() - 1)]
    far += [("centroid", bit) for bit in range(1, columns.bit_length() - 1)]
    by_line, by_column = across("line", 1), across("centroid", 0)
    turned, straight = by_parity(by_line, by_column), by_parity(by_column, by_line)

    distant = moved(centroids, across(*far[-1]))
    near = moved(centroids, straight)
    level = doubled([centroids], far[:-1])[1:]
    packed = pack(counts, own, partner, slots, block_rows)
    norms = line_norms(packed, slots)
    empty = jnp.full((2 * SUBLANES, own.shape[0]), HUGE_DISTANCE, jnp.float32)
    distant, counts = lax.optimization_barrier((distant, counts))
    beyond = doubled([distant], far[:-1])[1:]
    level, partner = lax.optimization_barrier((level, partner))
    near_level = moved(stacked([*level, distant]), straight)
    crossed_level = moved(stacked([centroids, near, *level, distant]), turned)
    near_beyond = moved(stacked([*beyond]), straight)
    lines = (packed, partner)
    states = (empty, empty)
    to_turned = stacked([near_level, *beyond])
    crossed_beyond = moved(to_turned, turned)
    near_last = near_beyond
    near_last, norms = lax.optimization_barrier((near_last, norms))
    corner = moved(near_last, turned)
    states = absorb(states, (centroids, near, *level, distant, near_level), lines)
    states = absorb(states, (near_beyond, *beyond, crossed_level), lines)
    mine, theirs = absorb(states, (crossed_beyond,), lines, give=True)
    returned = moved(theirs, partner_of)
    corner, mine = lax.optimization_barrier((corner, mine))
    banks = (corner, moved(corner, partner_of))

    placed = jnp.zeros((2, places, sub_rows), jnp.float32)
    sends = [None, None]
    for parity in (1, 0):
        placed, sends[parity] = last(
            parity,
            placed,
            counts,
            destinations,
            packed,
            banks,
            mine,
            returned,
            norms,
            block_rows,
        )
    to_even = moved(sends[1], lambda host, column: (host + 1, column))
    to_odd = moved(sends[0], partner_of)
    return tuple(final(merged(placed, to_even), to_odd))


def solution(mesh):
    in_specs = (P("line", "centroid", None), P("line"), P("line"), P(("centroid", "line"), None))
    out_specs = (P("line", "centroid"), P("line", "centroid"))
    return jax.shard_map(shards, mesh=mesh, in_specs=in_specs, out_specs=out_specs, check_vma=False)
```
